32 devices in a mesh: dp: 4 (over y, x), expert: 8 (over z, core).
Axes of the slice: x: 2, y: 2, z: 4, core: 2. Of those that a mesh axis runs over, the one named last changes fastest.
Arguments:
- tokens: bfloat16 [16384, 768], P(('dp', 'expert')), may hold values from -6 to 6
- cotangent: bfloat16 [16384, 768], P(('dp', 'expert')), may hold values from -6 to 6
- routes: int32 [16384, 2], P(('dp', 'expert')), may hold values from 0 to 3, all different within a row; in each aligned block of 512 rows (0 to 511, 512 to 1023, ...) at most 512 rows name the same one
- attention_weight: float32 [768, 3072], P('expert'), may hold values from -0.57735027 to 0.57735027
- attention_first: float32 [768, 3072], P('expert'), may hold values from -40 to 40
- attention_second: float32 [768, 3072], P('expert'), may hold values from 2.048 to 32.768
- router_weight: float32 [768, 4], P('expert'), may hold values from -0.375 to 0.375
- router_first: float32 [768, 4], P('expert'), may hold values from -768 to 768
- router_second: float32 [768, 4], P('expert'), may hold values from 566.231 to 9122.611
- norm_vectors: float32 [4, 768], P(None, 'expert'), may hold values from -0.3 to 1.3
- norm_first: float32 [4, 768], P(None, 'expert'), may hold values from -64 to 64
- norm_second: float32 [4, 768], P(None, 'expert'), may hold values from 4.096 to 65.536
- widen_weight: float32 [8, 768, 1536], P('expert', 'dp'), may hold values from -0.21875 to 0.21875
- widen_first: float32 [8, 768, 1536], P('expert', 'dp'), may hold values from -16 to 16
- widen_second: float32 [8, 768, 1536], P('expert', 'dp'), may hold values from 0.24576 to 4.096
- narrow_weight: float32 [8, 1536, 768], P('expert', 'dp'), may hold values from -0.21875 to 0.21875
- narrow_first: float32 [8, 1536, 768], P('expert', 'dp'), may hold values from -16 to 16
- narrow_second: float32 [8, 1536, 768], P('expert', 'dp'), may hold values from 0.36864 to 5.7344
Outputs:
- mixed: bfloat16 [16384, 768], P(('dp', 'expert'))
- tokens_grad: float32 [16384, 768], P(('dp', 'expert'))
- attention_mean: float32 [768, 3072], P('expert')
- attention_square: float32 [768, 3072], P('expert')
- attention_updated: float32 [768, 3072], P('expert')
- router_mean: float32 [768, 4], P('expert')
- router_square: float32 [768, 4], P('expert')
- router_updated: float32 [768, 4], P('expert')
- norm_mean: float32 [4, 768], P(None, 'expert')
- norm_square: float32 [4, 768], P(None, 'expert')
- norm_updated: float32 [4, 768], P(None, 'expert')
- widen_mean: float32 [8, 768, 1536], P('expert', 'dp')
- widen_square: float32 [8, 768, 1536], P('expert', 'dp')
- widen_updated: float32 [8, 768, 1536], P('expert', 'dp')
- narrow_mean: float32 [8, 1536, 768], P('expert', 'dp')
- narrow_square: float32 [8, 1536, 768], P('expert', 'dp')
- narrow_updated: float32 [8, 1536, 768], P('expert', 'dp')
The draws below stay inside these ranges and needn't reach their ends.
Inputs may be any that keep to these rules, and one draw needn't show every extreme that they name: `routes`: each row names two different experts; the rows of one device name one expert at most 512 times, a bound that some block reaches.
All inputs are finite; a program needn't handle non-finite values.
Results may differ from the reference program's by a relative error of at most 0.023.
Values may be sent and summed in bfloat16 or wider, within the bound.
No kernel may reach another device: no remote copies, remote signals or barrier semaphores. Data moves between devices by JAX's collectives and lax.ppermute only.
A program may use at most 256 MiB of HBM per device.

```python
import math
import jax
import jax.numpy as jnp
import numpy as np
from jax import lax

D = 768
HEADS = 12
HEAD_DIM = 64
FF = 3072
SEQ = 197
STEP = 5
TOK_DEV = 512
FF_PART = 1536
EXPERTS = 4
CAP = 512
GROUP = 4096
TOKENS = 16384
N_DP = 4
N_EXPERT = 8


def draw_attention_weight(key, part):
    key = jax.random.fold_in(key, 11)
    drawn = jax.random.truncated_normal(key, -4.0, 4.0, (D, 4 * D), jnp.float32)
    column = jnp.arange(4 * D)
    factor = jnp.where(column >= 3 * D, 4.0, 1.0) * D ** (-0.5)
    return (drawn * factor[None, :]).astype(jnp.float32)


def draw_norm_vectors(key, part):
    key = jax.random.fold_in(key, 12)
    drawn = jax.random.truncated_normal(key, -3.0, 3.0, (4, D), jnp.float32)
    is_gain = jnp.arange(4)[:, None] % 2 == 0
    return jnp.where(is_gain, 1.0 + 0.1 * drawn, 0.1 * drawn).astype(jnp.float32)


def with_spikes(array, rng, source, target, blocks, factor):
    def block_of(axis_at):
        return (jnp.arange(array.shape[axis_at]) // (array.shape[axis_at] // blocks)).reshape((-1,) + (1,) * (array.ndim - 1 - axis_at))

    one_side = jax.random.permutation(rng, blocks)[block_of(target)]
    other_side = (block_of(target) + blocks // 2) % blocks
    return jnp.where((block_of(source) == one_side) | (block_of(source) == other_side), factor * array, array)


def shard_levels(key, shape, split, smallest, top_value):
    def one(axis_at, blocks):
        draws = jax.random.uniform(jax.random.fold_in(jax.random.fold_in(key, 6), axis_at), (blocks,), jnp.float32, smallest / len(split), top_value / len(split))
        return jnp.repeat(jnp.exp(draws), shape[axis_at] // blocks).reshape((-1,) + (1,) * (len(shape) - axis_at - 1))

    loudness = one(*split[0])
    for cut in split[1:]:
        loudness = loudness * one(*cut)
    return loudness


def routed_block(key, own, number, rows, amount, top, most, lean):
    sequence = jax.random.permutation(key, amount)
    crowded, common = load_shares(amount, rows * top, most, lean, True), load_shares(amount, rows * top, most, lean, False)
    places = jnp.arange(amount)

    def named(sizes, turn):
        used = int((sizes > 0).sum())
        fixed = max(1, used // 4)
        shifted = fixed + (places - fixed + turn * (used - fixed)) % max(1, amount - fixed)
        return jnp.zeros((amount,), jnp.int32).at[sequence[jnp.where(places < fixed, places, shifted)]].set(jnp.asarray(sizes, jnp.int32))

    sizes = jnp.where(number % 4 == 0, named(crowded, number // 4), named(common, number - number // 4 - 1))
    mixed = jax.random.permutation(jax.random.fold_in(own, 3), amount)
    giver, sink = mixed[0:amount // 2 * 2:2], mixed[1:amount // 2 * 2:2]
    margin = jnp.minimum(sizes[giver] - 1, most - sizes[sink]) // 2
    margin = jnp.where((giver == sequence[0]) | (sink == sequence[0]) | (sizes[sink] == 0), 0, jnp.maximum(margin, 0))
    shifted = jax.random.randint(jax.random.fold_in(own, 4), (amount // 2,), 0, 1 << 20) % (margin + 1)
    sizes = sizes.at[giver].add(-shifted).at[sink].add(shifted)
    items = jnp.searchsorted(jnp.cumsum(sizes), jnp.arange(rows * top), side="right").astype(jnp.int32)
    listing = items.reshape(top, rows).T
    listing = listing[jax.random.permutation(jax.random.fold_in(own, 1), rows)]
    turn = jax.random.randint(jax.random.fold_in(own, 2), (rows, 1), 0, top)
    return jnp.take_along_axis(listing, (jnp.arange(top)[None, :] + turn) % top, axis=1)


def load_shares(number_of, total, bound, skew, full):
    loads = [(1 << 20) // math.isqrt(rank ** skew) + 1 for rank in range(1, number_of + 1)]
    largest = bound if full else min(bound, max(-(-total // number_of), total * loads[0] // sum(loads)))
    least = 1 if total - largest >= number_of - 1 else 0
    holding, spare = [largest] + [least] * (number_of - 1), total - largest - least * (number_of - 1)
    while spare > 0:
        movable = [i for i in range(1, number_of) if holding[i] < largest] or [i for i in range(1, number_of) if holding[i] < bound]
        mass, remaining = sum([loads[i] for i in movable]), spare
        for i in movable:
            addition = min(bound - holding[i], max(1, remaining * loads[i] // mass), spare)
            holding[i] = holding[i] + addition
            spare = spare - addition
    return np.array(holding)


def normal_values(own_key, shape, scale, reach, split=(), kind=jnp.bfloat16):
    values = scale * jax.random.normal(own_key, shape, jnp.float32)
    if split:
        values = values * shard_levels(own_key, shape, split, -0.22, 0.18)
    return jnp.clip(values, -reach, reach).astype(kind)


def noise_with(stream_key, extent, scale, reach, shards, heavy, kind=jnp.bfloat16):
    array = scale * jax.random.normal(stream_key, extent, jnp.float32)
    if shards:
        array = array * shard_levels(stream_key, extent, shards, -0.22, 0.18)
    return jnp.clip(with_spikes(array, jax.random.fold_in(stream_key, 3), *heavy), -reach, reach).astype(kind)


def setup_inputs(seed: int = 0) -> dict:
    arg_keys = jax.random.split(jax.random.key(seed), 19)
    tokens = normal_values(arg_keys[0], (TOKENS, D), 1.0, 6.0, ((0, 32),))
    cotangent = noise_with(arg_keys[1], (TOKENS, D), 1.0, 6.0, ((0, 32),), (0, 1, 32, 2.75))
    routes_keys = jax.random.split(jax.random.fold_in(arg_keys[2], 1), TOKENS // TOK_DEV)
    routes_turns = jax.random.permutation(jax.random.fold_in(arg_keys[2], 3), TOKENS // TOK_DEV)
    routes = jax.vmap(lambda own, number: routed_block(jax.random.fold_in(arg_keys[2], 2), own, number, TOK_DEV, EXPERTS, 2, CAP, 1))(routes_keys, routes_turns).reshape((TOKENS, 2))
    attention_weight = draw_attention_weight(jax.random.fold_in(arg_keys[18], 71), 0)
    attention_first = normal_values(arg_keys[4], (D, 4 * D), (TOKENS ** 0.5 / 18), 40.0, ((0, 8),), jnp.float32)
    attention_second = jnp.clip(jnp.exp(math.log(32.768) - 2.7725887 * jax.random.uniform(arg_keys[5], (D, 4 * D), jnp.float32) ** shard_levels(arg_keys[5], (D, 4 * D), ((0, 8),), -0.2, 0.2)), 2.048, 32.768)
    router_weight = normal_values(arg_keys[6], (D, EXPERTS), (0.75 * D ** -0.5), 0.375, ((0, 8),), jnp.float32)
    router_first = normal_values(arg_keys[7], (D, EXPERTS), (0.067 * (D * TOKENS // EXPERTS) ** 0.5), 768.0, ((0, 8),), jnp.float32)
    router_second = jnp.clip(jnp.exp(math.log(9122.611) - 2.7795092 * jax.random.uniform(arg_keys[8], (D, EXPERTS), jnp.float32) ** shard_levels(arg_keys[8], (D, EXPERTS), ((0, 8),), -0.2, 0.2)), 566.231, 9122.611)
    norm_vectors = draw_norm_vectors(jax.random.fold_in(arg_keys[18], 71), 0)
    norm_first = normal_values(arg_keys[10], (4, D), (0.08 * TOKENS ** 0.5), 64.0, ((1, 8),), jnp.float32)
    norm_second = jnp.clip(jnp.exp(math.log(65.536) - 2.7725887 * jax.random.uniform(arg_keys[11], (4, D), jnp.float32) ** shard_levels(arg_keys[11], (4, D), ((1, 8),), -0.2, 0.2)), 4.096, 65.536)
    widen_weight = normal_values(arg_keys[12], (N_EXPERT, D, FF_PART), D ** -0.5, 0.21875, ((0, 8), (1, 4)), jnp.float32)
    widen_first = normal_values(arg_keys[13], (N_EXPERT, D, FF_PART), (0.04 * (TOKENS // EXPERTS) ** 0.5), 16.0, ((0, 8), (1, 4)), jnp.float32)
    widen_second = jnp.clip(jnp.exp(math.log(4.096) - 2.8134108 * jax.random.uniform(arg_keys[14], (N_EXPERT, D, FF_PART), jnp.float32) ** shard_levels(arg_keys[14], (N_EXPERT, D, FF_PART), ((0, 8), (1, 4)), -0.2, 0.2)), 0.24576, 4.096)
    narrow_weight = normal_values(arg_keys[15], (N_EXPERT, FF_PART, D), (FF // 4) ** -0.5, 0.21875, ((0, 8), (1, 4)), jnp.float32)
    narrow_first = normal_values(arg_keys[16], (N_EXPERT, FF_PART, D), (0.047 * (TOKENS // EXPERTS) ** 0.5), 16.0, ((0, 8), (1, 4)), jnp.float32)
    narrow_second = jnp.clip(jnp.exp(math.log(5.7344) - 2.744418 * jax.random.uniform(arg_keys[17], (N_EXPERT, FF_PART, D), jnp.float32) ** shard_levels(arg_keys[17], (N_EXPERT, FF_PART, D), ((0, 8), (1, 4)), -0.2, 0.2)), 0.36864, 5.7344)
    return dict(tokens=tokens, cotangent=cotangent, routes=routes, attention_weight=attention_weight, attention_first=attention_first, attention_second=attention_second, router_weight=router_weight, router_first=router_first, router_second=router_second, norm_vectors=norm_vectors, norm_first=norm_first, norm_second=norm_second, widen_weight=widen_weight, widen_first=widen_first, widen_second=widen_second, narrow_weight=narrow_weight, narrow_first=narrow_first, narrow_second=narrow_second)


HIGHEST = lax.Precision.HIGHEST
NORM_EPS = 1e-06
SCORE_SCALE = 0.125
MASKED = -1000000000.0
BETA_ONE = 0.9
BETA_TWO = 0.999
ADAM_EPS = 1e-08
MATRIX_RATE = 0.04
VECTOR_RATE = 0.2
DECAY = 0.1

@jax.custom_vjp
def low(v):
    return lax.optimization_barrier(v.astype(jnp.bfloat16)).astype(jnp.float32)

@jax.custom_vjp
def low_back(v):
    return v

def low_keep(v):
    return (low(v), None)

def low_pass(kept, grad):
    return (grad,)

def back_keep(v):
    return (v, None)

def back_low(kept, grad):
    return (low(grad),)
low.defvjp(low_keep, low_pass)
low_back.defvjp(back_keep, back_low)

def layer_norm(values, norm_gain, norm_shift):
    center = values - lax.optimization_barrier(jnp.mean(values, axis=-1, keepdims=True))
    spread = lax.optimization_barrier(jnp.mean(center * center, axis=-1, keepdims=True))
    return center * lax.rsqrt(spread + NORM_EPS) * norm_gain + norm_shift

def matmul(left, right):
    return jnp.dot(left, right, precision=HIGHEST)

def group_attention(queries, all_keys, all_values):
    group_rows = queries.shape[0]
    rim = SEQ - 1
    span = TOK_DEV + 2 * rim
    keys_pad = jnp.pad(all_keys, ((rim, rim), (0, 0)))
    values_pad = jnp.pad(all_values, ((rim, rim), (0, 0)))

    def one_block(offset):
        query_blk = lax.dynamic_slice_in_dim(queries, offset, TOK_DEV, 0).reshape(TOK_DEV, HEADS, HEAD_DIM)
        key_blk = lax.dynamic_slice_in_dim(keys_pad, offset, span, 0).reshape(span, HEADS, HEAD_DIM)
        value_blk = lax.dynamic_slice_in_dim(values_pad, offset, span, 0).reshape(span, HEADS, HEAD_DIM)
        query_rows = offset + jnp.arange(TOK_DEV, dtype=jnp.int32)
        key_rows = offset - rim + jnp.arange(span, dtype=jnp.int32)
        allowed = (query_rows[:, None] // SEQ == key_rows[None, :] // SEQ) & (key_rows[None, :] >= 0) & (key_rows[None, :] < group_rows)
        scores = low_back(jnp.einsum('qhd,khd->hqk', query_blk, key_blk, precision=HIGHEST) * SCORE_SCALE)
        scores = jnp.where(allowed[None], scores, MASKED)
        peak = lax.optimization_barrier(jnp.max(scores, axis=-1, keepdims=True))
        raised = jnp.exp(scores - peak)
        attend = raised / lax.optimization_barrier(jnp.sum(raised, axis=-1, keepdims=True))
        heads = jnp.einsum('hqk,khd->qhd', low(attend), value_blk, precision=HIGHEST)
        return heads.reshape(TOK_DEV, HEADS * HEAD_DIM)
    offsets = jnp.arange(group_rows // TOK_DEV, dtype=jnp.int32) * TOK_DEV
    return lax.map(jax.checkpoint(one_block), offsets).reshape(group_rows, HEADS * HEAD_DIM)

def one_expert(items):
    block, widen_pair, narrow_pair = items
    before_act = low_back(jnp.einsum('rd,hdf->hrf', block, widen_pair, precision=HIGHEST))
    act_low = low(jax.nn.gelu(before_act, approximate=False))
    parts = low(low_back(jnp.einsum('hrf,hfd->hrd', act_low, narrow_pair, precision=HIGHEST)))
    return parts[0] + parts[1]

def group_experts(rows, group_routes, widen_low, narrow_low):
    flat = group_routes.reshape(N_EXPERT, 2 * TOK_DEV)
    table = (flat[:, :, None] == jnp.arange(EXPERTS, dtype=jnp.int32)[None, None, :]).astype(jnp.int32)
    before = jnp.cumsum(table, axis=1) - table
    slots = lax.optimization_barrier(jnp.sum(before * table, axis=2)) + jnp.arange(N_EXPERT, dtype=jnp.int32)[:, None] * CAP
    expert_ids = flat.reshape(-1)
    slot_ids = slots.reshape(-1)
    doubled = jnp.repeat(rows, 2, axis=0)
    buffer = jnp.zeros((EXPERTS, N_EXPERT * CAP, D), jnp.float32).at[expert_ids, slot_ids].set(doubled)
    outputs = lax.map(jax.checkpoint(one_expert), (buffer, widen_low.reshape(EXPERTS, 2, D, FF_PART), narrow_low.reshape(EXPERTS, 2, FF_PART, D)))
    return outputs[expert_ids, slot_ids].reshape(GROUP, 2, D)

def forward(tokens_float, routes, attention_weight, router_weight, norm_vectors, widen_weight, narrow_weight):
    attention_low = low(attention_weight)
    router_low = low(router_weight)
    norm_low = low(norm_vectors)
    widen_low = low(widen_weight)
    narrow_low = low(narrow_weight)
    hidden_one = low(layer_norm(tokens_float, norm_low[0], norm_low[1]))
    triple = low(low_back(matmul(hidden_one, attention_low[:, :3 * D])))
    heads_all = []
    for group_index in range(N_DP):
        rows_here = triple[group_index * GROUP:(group_index + 1) * GROUP]
        heads_all.append(group_attention(rows_here[:, :D], rows_here[:, D:2 * D], rows_here[:, 2 * D:]))
    heads_low = low(low_back(jnp.concatenate(heads_all, axis=0)))
    resid = tokens_float + low_back(matmul(heads_low, attention_low[:, 3 * D:]))
    hidden_two = low(layer_norm(resid, norm_low[2], norm_low[3]))
    logits = matmul(hidden_two, router_low)
    chooser = (routes[:, :, None] == jnp.arange(EXPERTS, dtype=jnp.int32)[None, None, :]).astype(jnp.float32)
    chosen = lax.optimization_barrier(jnp.sum(chooser * logits[:, None, :], axis=-1))
    peak = lax.optimization_barrier(jnp.max(chosen, axis=-1, keepdims=True))
    raised = jnp.exp(chosen - peak)
    gates = raised / lax.optimization_barrier(jnp.sum(raised, axis=-1, keepdims=True))
    combined_all = []
    for group_index in range(N_DP):
        lower_row = group_index * GROUP
        combined_all.append(group_experts(hidden_two[lower_row:lower_row + GROUP], routes[lower_row:lower_row + GROUP], widen_low, narrow_low))
    combined = jnp.concatenate(combined_all, axis=0)
    return resid + lax.optimization_barrier(jnp.sum(gates[:, :, None] * combined, axis=1))

def adam_step(weight, first, second, grad, rate, decay):
    new_first = BETA_ONE * first + (1.0 - BETA_ONE) * grad
    new_second = BETA_TWO * second + (1.0 - BETA_TWO) * grad * grad
    mean_hat = new_first / (1.0 - BETA_ONE ** STEP)
    square_hat = new_second / (1.0 - BETA_TWO ** STEP)
    updated = weight - rate * (mean_hat / (jnp.sqrt(square_hat) + ADAM_EPS) + decay * weight)
    return (new_first, new_second, updated)

def reference(tokens, cotangent, routes, attention_weight, attention_first, attention_second, router_weight, router_first, router_second, norm_vectors, norm_first, norm_second, widen_weight, widen_first, widen_second, narrow_weight, narrow_first, narrow_second):
    tokens_float = tokens.astype(jnp.float32)

    def closed(token_rows, attention_w, router_w, norm_w, widen_w, narrow_w):
        return forward(token_rows, routes, attention_w, router_w, norm_w, widen_w, narrow_w)
    output, pull = jax.vjp(closed, tokens_float, attention_weight, router_weight, norm_vectors, widen_weight, narrow_weight)
    grads = pull(cotangent.astype(jnp.float32))
    attention_new = adam_step(attention_weight, attention_first, attention_second, grads[1], MATRIX_RATE, DECAY)
    router_new = adam_step(router_weight, router_first, router_second, grads[2], MATRIX_RATE, DECAY)
    norm_new = adam_step(norm_vectors, norm_first, norm_second, grads[3], VECTOR_RATE, 0.0)
    widen_new = adam_step(widen_weight, widen_first, widen_second, grads[4], MATRIX_RATE, DECAY)
    narrow_new = adam_step(narrow_weight, narrow_first, narrow_second, grads[5], MATRIX_RATE, DECAY)
    return (output.astype(jnp.bfloat16), grads[0], attention_new[0], attention_new[1], attention_new[2], router_new[0], router_new[1], router_new[2], norm_new[0], norm_new[1], norm_new[2], widen_new[0], widen_new[1], widen_new[2], narrow_new[0], narrow_new[1], narrow_new[2])
```

```python
import functools

import jax
import jax.numpy as jnp
from jax import lax
from jax.experimental import pallas as pl
from jax.experimental.pallas import tpu as pltpu
from jax.sharding import PartitionSpec as P

HEADS = 12
HEAD_DIM = 64
SEQ = 197
STEP = 5

HIGHEST = lax.Precision.HIGHEST
NORM_EPS = 1e-06
SCORE_SCALE = 0.125
MASKED = -1000000000.0
BETA_ONE = 0.9
BETA_TWO = 0.999
ADAM_EPS = 1e-08
MATRIX_RATE = 0.04
VECTOR_RATE = 0.2
DECAY = 0.1

F32 = jnp.float32
BF16 = jnp.bfloat16
LANES = 128
HALO = 256
QUERY_TILE = 256
ROW_TILE = 256
VMEM_LIMIT = 56 * 1024 * 1024
EXTRA = 16
EXPERT_VMEM = 32 * 1024 * 1024


def tie_kernel(*refs):
    pass


def tie(block, *dependencies):
    anywhere = pl.BlockSpec(memory_space=pl.ANY)
    return pl.pallas_call(
        tie_kernel,
        out_shape=jax.ShapeDtypeStruct(block.shape, block.dtype),
        in_specs=[anywhere] * (1 + len(dependencies)),
        out_specs=anywhere,
        input_output_aliases={0: 0},
        name="tie",
    )(block, *dependencies)


def hop(block, distance):
    count = lax.axis_size("expert")
    return lax.ppermute(block, "expert", [(i, (i + distance) % count) for i in range(count)])


def ring(block):
    return hop(block, 2)


def pair(block):
    return lax.ppermute(block, "expert", [(i, i ^ 1) for i in range(lax.axis_size("expert"))])


def across(block, bit):
    return lax.ppermute(block, "dp", [(i, i ^ bit) for i in range(lax.axis_size("dp"))])


def place_kernel(index, block, *refs):
    refs[-1][0] = block[...]


def place(out, count, block, index):
    anywhere = [pl.BlockSpec(memory_space=pl.ANY)]
    half = (block.shape[0] // 2,) + block.shape[1:]
    return pl.pallas_call(
        place_kernel,
        grid_spec=pltpu.PrefetchScalarGridSpec(
            num_scalar_prefetch=1,
            grid=(2,),
            in_specs=[pl.BlockSpec(half, lambda i, t: (i, 0))] + ([] if out is None else anywhere),
            out_specs=pl.BlockSpec((1,) + half, lambda i, t: (t[0], i, 0)),
        ),
        out_shape=jax.ShapeDtypeStruct((count,) + block.shape, block.dtype),
        input_output_aliases={} if out is None else {2: 0},
        cost_estimate=pl.CostEstimate(
            flops=0, bytes_accessed=2 * block.size * block.dtype.itemsize, transcendentals=0
        ),
        name="place",
    )(*((index.reshape(1), block) + (() if out is None else (out,))))


def gather_dp_near(block):
    count = lax.axis_size("dp")
    if count != 4:
        return lax.all_gather(block, "dp", axis=0), None
    me = lax.axis_index("dp")
    out = place(None, count, block, me)
    for bits in (1, 2):
        out = place(out, count, across(block, bits), me ^ bits)
    return out, across(block, 3)


def gather_dp_far(out, far):
    return out if far is None else place(out, out.shape[0], far, lax.axis_index("dp") ^ 3)


def added(*parts):
    total = parts[0].astype(F32)
    for part in parts[1:]:
        total = total + part.astype(F32)
    return total


def scatter_dp_start(parts):
    one, two = lax.axis_index("dp") % 2, lax.axis_index("dp") // 2
    half = parts.shape[1] // 2
    grid = parts.reshape((2, 2) + parts.shape[1:])
    first, second = grid[:, :, :half], grid[:, :, half:]
    first_got = across(lax.dynamic_index_in_dim(first, 1 - one, 1, False), 1)
    second_got = across(lax.dynamic_index_in_dim(second, 1 - two, 0, False), 2)
    return first, second, first_got, second_got


def scatter_dp_middle(state, then):
    one, two = lax.axis_index("dp") % 2, lax.axis_index("dp") // 2
    first, second, first_got, second_got = state
    first_got, second_got = tie(first_got, then), tie(second_got, then)
    first_sum = added(lax.dynamic_index_in_dim(first, one, 1, False), first_got).astype(BF16)
    second_sum = added(lax.dynamic_index_in_dim(second, two, 0, False), second_got).astype(BF16)
    first_got = across(lax.dynamic_index_in_dim(first_sum, 1 - two, 0, False), 2)
    second_got = across(lax.dynamic_index_in_dim(second_sum, 1 - one, 0, False), 1)
    return first_sum, second_sum, first_got, second_got


def scatter_dp_end(state, then):
    one, two = lax.axis_index("dp") % 2, lax.axis_index("dp") // 2
    first_sum, second_sum, first_got, second_got = state
    first_got, second_got = tie(first_got, then), tie(second_got, then)
    first_sum = added(lax.dynamic_index_in_dim(first_sum, two, 0, False), first_got)
    second_sum = added(lax.dynamic_index_in_dim(second_sum, one, 0, False), second_got)
    return jnp.concatenate([first_sum, second_sum], axis=0)


def gather_expert(block, by_hops):
    count = lax.axis_size("expert")
    if not by_hops:
        return lax.all_gather(block, "expert", axis=0)
    chip, core = lax.axis_index("expert") // 2, lax.axis_index("expert") % 2
    given = pair(block)
    both = jnp.where(core == 0, jnp.stack([block, given]), jnp.stack([given, block]))
    blocks = [both] + [hop(both, 2 * step) for step in range(1, count // 2)]
    pieces = []
    for place in range(count // 2):
        piece = blocks[0]
        for step in range(1, count // 2):
            piece = jnp.where((place + step) % (count // 2) == chip, blocks[step], piece)
        pieces.append(piece)
    return jnp.concatenate(pieces, axis=0)


def sum_to_owner(cut, then=(None, None, None, None)):
    replicas, chips = cut.shape[1], cut.shape[2]
    chip, core = lax.axis_index("expert") // 2, lax.axis_index("expert") % 2
    me = lax.axis_index("dp")

    def held(got, place):
        return got if then[place] is None else [tie(got[0], then[place])] + got[1:]

    got = held([pair(lax.dynamic_index_in_dim(cut, 1 - core, 0, False))], 0)
    over_pair = added(lax.dynamic_index_in_dim(cut, core, 0, False), *got).astype(BF16)
    got = [
        across(lax.dynamic_index_in_dim(over_pair, me ^ bits, 0, False), bits)
        for bits in range(1, replicas)
    ]
    got = held(got, 1)
    over_dp = added(lax.dynamic_index_in_dim(over_pair, me, 0, False), *got).astype(BF16)
    got = [
        hop(lax.dynamic_index_in_dim(over_dp, (chip + step) % chips, 0, False), 2 * step)
        for step in range(1, chips)
    ]
    got = held(got, 2)
    owned = added(lax.dynamic_index_in_dim(over_dp, chip, 0, False), *got).astype(BF16)
    got = held([across(owned, bits) for bits in range(1, replicas)], 3)
    blocks = [owned] + got
    pieces = []
    for place in range(replicas):
        piece = blocks[0]
        for bits in range(1, replicas):
            piece = jnp.where(place ^ bits == me, blocks[bits], piece)
        pieces.append(piece.astype(F32))
    return jnp.concatenate(pieces, axis=0), (over_pair, over_dp, owned)


def standardised(values):
    center = values - jnp.mean(values, axis=-1, keepdims=True)
    spread = jnp.mean(center * center, axis=-1, keepdims=True)
    inverse = lax.rsqrt(spread + NORM_EPS)
    return center * inverse, inverse


def norm_pull(grad, unit, inverse, gain):
    scaled = grad * gain
    mean = jnp.mean(scaled, axis=-1, keepdims=True)
    along = jnp.mean(scaled * unit, axis=-1, keepdims=True)
    return inverse * (scaled - mean - unit * along)


def exact_gelu(values):
    return jax.nn.gelu(values, approximate=False)


def adam_step(weight, first, second, grad, rate, decay):
    new_first = BETA_ONE * first + (1.0 - BETA_ONE) * grad
    new_second = BETA_TWO * second + (1.0 - BETA_TWO) * grad * grad
    mean_hat = new_first / (1.0 - BETA_ONE**STEP)
    square_hat = new_second / (1.0 - BETA_TWO**STEP)
    updated = weight - rate * (mean_hat / (jnp.sqrt(square_hat) + ADAM_EPS) + decay * weight)
    return (new_first, new_second, updated)


def dot_nt(left, right):
    return lax.dot_general(left, right, (((1,), (1,)), ((), ())), preferred_element_type=F32)


def dot_tn(left, right):
    return lax.dot_general(left, right, (((0,), (0,)), ((), ())), preferred_element_type=F32)


def dot_nn(left, right):
    return jnp.dot(left, right, preferred_element_type=F32)


def head_lanes(head):
    lane = lax.broadcasted_iota(jnp.int32, (1, LANES), 1)
    return (lane // HEAD_DIM) == head


def attend_kernel(query_image, key_image, q_ref, k_ref, v_ref, out_ref):
    rows = out_ref.shape[0]
    window = QUERY_TILE + 2 * HALO
    for tile in range(rows // QUERY_TILE):
        low = tile * QUERY_TILE
        queries = q_ref[HALO + low : HALO + low + QUERY_TILE, :] * SCORE_SCALE
        keys = k_ref[low : low + window, :]
        values = v_ref[low : low + window, :]
        allowed = query_image[low : low + QUERY_TILE, :] == key_image[:, low : low + window]
        result = None
        for head in range(LANES // HEAD_DIM):
            lanes = head_lanes(head)
            scores = dot_nt(jnp.where(lanes, queries, 0).astype(BF16), keys)
            scores = jnp.where(allowed, scores, MASKED)
            raised = jnp.exp(scores - jnp.max(scores, axis=-1, keepdims=True))
            attend = raised * (1.0 / jnp.sum(raised, axis=-1, keepdims=True))
            found = dot_nn(attend.astype(BF16), values)
            result = found if result is None else jnp.where(lanes, found, result)
        out_ref[low : low + QUERY_TILE, :] = result.astype(BF16)


def attention(triple, query_image, key_image):
    span = triple.shape[0]
    rows = span - 2 * HALO
    width = triple.shape[1] // 3
    blocks = width // LANES
    cost = HEADS * rows * (QUERY_TILE + 2 * HALO)
    return pl.pallas_call(
        attend_kernel,
        grid=(blocks,),
        in_specs=[
            pl.BlockSpec((rows, 1), lambda i: (0, 0)),
            pl.BlockSpec((1, span), lambda i: (0, 0)),
            pl.BlockSpec((span, LANES), lambda i: (0, i)),
            pl.BlockSpec((span, LANES), lambda i: (0, blocks + i)),
            pl.BlockSpec((span, LANES), lambda i: (0, 2 * blocks + i)),
        ],
        out_specs=pl.BlockSpec((rows, LANES), lambda i: (0, i)),
        out_shape=jax.ShapeDtypeStruct((rows, width), BF16),
        compiler_params=pltpu.CompilerParams(vmem_limit_bytes=VMEM_LIMIT),
        cost_estimate=pl.CostEstimate(
            flops=cost * 512, bytes_accessed=span * width * 6, transcendentals=cost
        ),
        name="attention",
    )(query_image[:, None], key_image[None, :], triple, triple, triple)


def attend_back_kernel(query_image, key_image, q_ref, k_ref, v_ref, g_ref, out_ref, dk, dv):
    rows = g_ref.shape[0]
    span = k_ref.shape[0]
    width = out_ref.shape[1] // 3
    window = QUERY_TILE + 2 * HALO
    column = pl.program_id(0) * LANES

    def columns(part):
        return pl.ds(pl.multiple_of(part * width + column, LANES), LANES)

    dk[...] = jnp.zeros_like(dk)
    dv[...] = jnp.zeros_like(dv)
    out_ref[:HALO, columns(0)] = jnp.zeros((HALO, LANES), BF16)
    out_ref[span - HALO :, columns(0)] = jnp.zeros((HALO, LANES), BF16)
    for tile in range(rows // QUERY_TILE):
        low = tile * QUERY_TILE
        queries = q_ref[HALO + low : HALO + low + QUERY_TILE, :] * SCORE_SCALE
        grads = g_ref[low : low + QUERY_TILE, :]
        keys = k_ref[low : low + window, :]
        values = v_ref[low : low + window, :]
        allowed = key_image[low : low + window, :] == query_image[:, low : low + QUERY_TILE]
        query_grad = None
        for head in range(LANES // HEAD_DIM):
            lanes = head_lanes(head)
            own_queries = jnp.where(lanes, queries, 0).astype(BF16)
            own_grads = jnp.where(lanes, grads, 0).astype(BF16)
            scores = jnp.where(allowed, dot_nt(keys, own_queries), MASKED)
            raised = jnp.exp(scores - jnp.max(scores, axis=0, keepdims=True))
            attend = raised * (1.0 / jnp.sum(raised, axis=0, keepdims=True))
            dv[low : low + window, :] += dot_nn(attend.astype(BF16), own_grads)
            pulled = dot_nt(values, own_grads)
            inner = jnp.sum(attend * pulled, axis=0, keepdims=True)
            score_grad = (attend * (pulled - inner)).astype(BF16)
            dk[low : low + window, :] += dot_nn(score_grad, own_queries)
            found = dot_tn(score_grad, keys) * SCORE_SCALE
            query_grad = found if query_grad is None else jnp.where(lanes, found, query_grad)
        out_ref[HALO + low : HALO + low + QUERY_TILE, columns(0)] = query_grad.astype(BF16)
    out_ref[:, columns(1)] = dk[...].astype(BF16)
    out_ref[:, columns(2)] = dv[...].astype(BF16)


def attention_back(triple, grads, query_image, key_image):
    span = triple.shape[0]
    rows = span - 2 * HALO
    width = triple.shape[1] // 3
    blocks = width // LANES
    cost = HEADS * rows * (QUERY_TILE + 2 * HALO)
    return pl.pallas_call(
        attend_back_kernel,
        grid=(blocks,),
        in_specs=[
            pl.BlockSpec((1, rows), lambda i: (0, 0)),
            pl.BlockSpec((span, 1), lambda i: (0, 0)),
            pl.BlockSpec((span, LANES), lambda i: (0, i)),
            pl.BlockSpec((span, LANES), lambda i: (0, blocks + i)),
            pl.BlockSpec((span, LANES), lambda i: (0, 2 * blocks + i)),
            pl.BlockSpec((rows, LANES), lambda i: (0, i)),
        ],
        out_specs=pl.BlockSpec((span, 3 * width), lambda i: (0, 0)),
        out_shape=jax.ShapeDtypeStruct((span, 3 * width), BF16),
        scratch_shapes=[pltpu.VMEM((span, LANES), F32), pltpu.VMEM((span, LANES), F32)],
        compiler_params=pltpu.CompilerParams(vmem_limit_bytes=VMEM_LIMIT),
        cost_estimate=pl.CostEstimate(
            flops=cost * 1280, bytes_accessed=span * width * 14, transcendentals=cost
        ),
        name="attention_back",
    )(query_image[None, :], key_image[:, None], triple, triple, triple, grads)


def first_norm_kernel(below, tokens, above, vectors, out):
    low = 0
    for block in (below, tokens, above):
        unit, _ = standardised(block[...].astype(F32))
        out[low : low + block.shape[0], :] = (unit * vectors[0:1] + vectors[1:2]).astype(BF16)
        low += block.shape[0]


def first_norm(below, tokens, above, vectors):
    span, width = tokens.shape[0] + 2 * HALO, tokens.shape[1]
    return pl.pallas_call(
        first_norm_kernel,
        out_shape=jax.ShapeDtypeStruct((span, width), BF16),
        compiler_params=pltpu.CompilerParams(vmem_limit_bytes=VMEM_LIMIT),
        cost_estimate=pl.CostEstimate(
            flops=span * width * 10, bytes_accessed=span * width * 4, transcendentals=0
        ),
        name="first_norm",
    )(below, tokens, above, vectors)


def dense_back_kernel(
    layout, hidden, below, tokens, above, grads, weight, small, dense_out, back_out
):
    cores, replicas, chips, rows = layout
    width = hidden.shape[1]
    gain = jnp.zeros((1, width), F32)
    shift = jnp.zeros((1, width), F32)
    low = 0
    for block in (below, tokens, above):
        here = slice(low, low + block.shape[0])
        back = dot_nt(grads[here, :], weight[...])
        back_out[here, :] = back.astype(BF16)
        unit, _ = standardised(block[...].astype(F32))
        gain += jnp.sum(back * unit, axis=0, keepdims=True)
        shift += jnp.sum(back, axis=0, keepdims=True)
        low += block.shape[0]
    sums = jnp.concatenate(
        [
            gain,
            shift,
            jnp.zeros((6, width), F32),
        ],
        axis=0,
    )
    lane = lax.broadcasted_iota(jnp.int32, (8, LANES), 1)
    row = lax.broadcasted_iota(jnp.int32, (8, LANES), 0)
    spread = (lane == row).astype(F32)

    def store(low, block):
        for chip in range(chips):
            for core in range(cores):
                for replica in range(replicas):
                    start = ((chip * cores + core) * replicas + replica) * rows
                    piece = block[start : start + rows].astype(BF16)
                    dense_out[core, replica, chip, :, low : low + block.shape[1]] = piece

    for low in range(0, 3 * width, width):
        store(low, dot_tn(hidden[...], grads[:, low : low + width]))
    store(
        3 * width,
        lax.dot_general(
            small[...] + sums,
            spread,
            (((0,), (0,)), ((), ())),
            precision=HIGHEST,
            preferred_element_type=F32,
        ),
    )


def dense_back(hidden, below, tokens, above, grads, weight, small, layout):
    span, width = hidden.shape
    columns = 3 * width + LANES
    return pl.pallas_call(
        functools.partial(dense_back_kernel, layout),
        out_shape=[
            jax.ShapeDtypeStruct(layout + (columns,), BF16),
            jax.ShapeDtypeStruct((span, width), BF16),
        ],
        compiler_params=pltpu.CompilerParams(vmem_limit_bytes=VMEM_LIMIT),
        cost_estimate=pl.CostEstimate(
            flops=span * width * width * 12,
            bytes_accessed=span * width * 16 + width * width * 12,
            transcendentals=0,
        ),
        name="dense_back",
    )(hidden, below, tokens, above, grads, weight, small)


def small_adam_kernel(sums, *refs):
    values = [ref[...] for ref in refs[:6]]
    vectors, matrix = refs[0].shape[0], refs[3].shape[1]
    rows = sums.shape[0]
    lane = lax.broadcasted_iota(jnp.int32, (rows, rows), 1)
    row = lax.broadcasted_iota(jnp.int32, (rows, rows), 0)
    turned = lax.dot_general(
        sums[...],
        (lane == row).astype(F32),
        (((0,), (0,)), ((), ())),
        precision=HIGHEST,
        preferred_element_type=F32,
    )
    found = adam_step(*values[:3], turned[:vectors], VECTOR_RATE, 0.0)
    found += adam_step(
        *values[3:], sums[:, vectors : vectors + matrix], MATRIX_RATE, DECAY
    )
    for ref, value in zip(refs[6:], found):
        ref[...] = value


def small_adam(sums, *arrays):
    return pl.pallas_call(
        small_adam_kernel,
        out_shape=[jax.ShapeDtypeStruct(array.shape, F32) for array in arrays],
        name="small_adam",
    )(sums, *arrays)


def gelu_and_slope(values):
    inverse = 1.0 / (1.0 + (0.3275911 * 0.7071067811865476) * jnp.abs(values))
    fit = 1.061405429 * inverse - 1.453152027
    fit = fit * inverse + 1.421413741
    fit = fit * inverse - 0.284496736
    fit = fit * inverse + 0.254829592
    bell = jnp.exp(-0.5 * values * values)
    tail = (0.5 * fit) * (inverse * bell)
    share = jnp.where(values >= 0.0, 1.0 - tail, tail)
    return values * share, share + values * (bell * 0.3989422804014327)


def expert_kernel(first, target, rows_ref, grads_ref, gates, mark, place, weights, *refs):
    outs = refs if first else refs[5:]
    act_out, pre_out, part_out, rows_out, mixed_out, back_out = outs
    tile = pl.program_id(0)
    rows = rows_ref[...]
    gate = dot_tn(gates[...], mark[...])
    width = rows.shape[1]
    gate = jnp.concatenate([gate] * (width // LANES), axis=1)
    grads_float = grads_ref[...].astype(F32)
    grad_part = (gate * grads_float).astype(BF16)
    rows_out[...] = rows
    part_out[...] = grad_part
    part = None
    back = None
    replicas, parts, size = weights.shape
    quarter = parts // 4
    narrow_all = weights[:, 2 * quarter :, :].reshape(2 * size, width)
    for turn in range(2):
        here = slice(turn * size, (turn + 1) * size)
        widen = weights[:, turn * quarter : (turn + 1) * quarter, :].reshape(width, size)
        narrow = narrow_all[here, :]
        before = dot_nn(rows, widen)
        pulled = dot_nt(grad_part, narrow)
        act, slope = gelu_and_slope(before)
        act = act.astype(BF16)
        grad_pre = (pulled * slope).astype(BF16)
        act_out[:, here] = act
        pre_out[:, here] = grad_pre
        part_here = dot_nn(act, narrow)
        back_here = dot_nt(grad_pre, widen)
        part = part_here if part is None else part + part_here
        back = back_here if back is None else back + back_here
    part = part.astype(BF16).astype(F32)
    product = part * grads_float
    folded = product[:, :LANES]
    for low in range(LANES, width, LANES):
        folded = folded + product[:, low : low + LANES]
    dots = lax.dot_general(
        jnp.ones((EXTRA, LANES), F32),
        folded,
        (((1,), (1,)), ((), ())),
        precision=HIGHEST,
        preferred_element_type=F32,
    )
    high = dots.astype(BF16).astype(F32)
    dots = high * place[0] + (dots - high) * place[1]
    mixed_out[...] = (gate * part).astype(BF16)
    count = rows.shape[0]
    back_out[pl.ds(pl.multiple_of(tile * count, count), count), :] = back.astype(BF16)
    extra = slice(back_out.shape[0] - EXTRA, back_out.shape[0])
    back_out[extra, pl.ds(pl.multiple_of(tile * count, count), count)] = dots.astype(BF16)


def expert_block(place, places, target, payload, grads_block, marks, weights, kept):
    rows, width = grads_block.shape
    replicas, parts, _ = weights.shape
    hidden = parts * replicas // 2
    tiles = rows // ROW_TILE
    every = places * rows
    by_tile = pl.BlockSpec((ROW_TILE, width), lambda i, t: (i, 0))
    at = lambda i, t: (place * tiles + i, 0)
    whole = lambda i, t: (0, 0)
    first = kept is None
    kept = () if first else kept
    gate_mark, dot_mark = marks
    return pl.pallas_call(
        functools.partial(expert_kernel, first),
        grid_spec=pltpu.PrefetchScalarGridSpec(
            num_scalar_prefetch=1,
            grid=(tiles,),
            in_specs=[
                by_tile,
                by_tile,
                pl.BlockSpec((EXTRA, ROW_TILE), lambda i, t: (rows // EXTRA, i)),
                pl.BlockSpec((EXTRA, LANES), whole),
                pl.BlockSpec((2, EXTRA, 1), lambda i, t: (0, 0, 0)),
                pl.BlockSpec(
                    (replicas, parts, width), lambda i, t: (0, 0, 0), pipeline_mode=pl.Buffered(1)
                ),
            ]
            + [pl.BlockSpec(memory_space=pl.ANY)] * len(kept),
            out_specs=[
                pl.BlockSpec((ROW_TILE, hidden), at),
                pl.BlockSpec((ROW_TILE, hidden), at),
                pl.BlockSpec((ROW_TILE, width), at),
                pl.BlockSpec((ROW_TILE, width), at),
                pl.BlockSpec((ROW_TILE, width), lambda i, t: (t[0] * tiles + i, 0)),
                pl.BlockSpec((rows + EXTRA, width), whole),
            ],
        ),
        out_shape=[
            pltpu.HBM((every, hidden), BF16),
            pltpu.HBM((every, hidden), BF16),
            pltpu.HBM((every, width), BF16),
            pltpu.HBM((every, width), BF16),
            pltpu.HBM((every, width), BF16),
            jax.ShapeDtypeStruct((rows + EXTRA, width), BF16),
        ],
        input_output_aliases={7 + i: i for i in range(len(kept))},
        compiler_params=pltpu.CompilerParams(vmem_limit_bytes=EXPERT_VMEM),
        cost_estimate=pl.CostEstimate(
            flops=rows * width * hidden * 8,
            bytes_accessed=rows * (2 * hidden + 6 * width) * 2 + 4 * width * hidden,
            transcendentals=rows * hidden,
        ),
        name="expert_block",
    )(
        target.reshape(1),
        payload,
        grads_block,
        payload,
        gate_mark,
        dot_mark,
        weights,
        *kept,
    )


def split_float(values, terms):
    parts = []
    for _ in range(terms):
        part = lax.reduce_precision(values, 8, 7)
        parts.append(part.astype(BF16))
        values = values - part
    return parts


def experts_by_ring(hidden_two, gates, weights, next_grads, grads_mine):
    chips = lax.axis_size("expert") // 2
    expert_count, rows = gates.shape
    width = hidden_two.shape[1]
    chip, core = lax.axis_index("expert") // 2, lax.axis_index("expert") % 2
    number = jnp.arange(EXTRA, dtype=jnp.int32)[:, None]
    gate_mark = jnp.broadcast_to(
        (number % expert_count == chip) & (number < 3 * expert_count), (EXTRA, LANES)
    ).astype(BF16)
    slot = 2 * (core * expert_count + chip)
    dot_mark = jnp.stack([number == slot, number == slot + 1]).astype(F32)
    marks = (gate_mark, dot_mark)
    carried = jnp.pad(
        jnp.concatenate(split_float(gates, 3), axis=0),
        ((0, EXTRA - 3 * expert_count), (0, width - rows)),
    )
    kept = None
    carry = None
    backs = []
    mine = jnp.concatenate([hidden_two, carried], axis=0)
    for step in range(chips):
        other = pair(mine)
        if step + 1 < chips:
            following = ring(mine)
        source = (chip - step) % chips
        found_mine = expert_block(
            2 * step,
            2 * chips,
            2 * source + core,
            mine,
            grads_mine[step],
            marks,
            weights,
            kept,
        )
        found_other = expert_block(
            2 * step + 1,
            2 * chips,
            2 * source + 1 - core,
            other,
            pair(grads_mine[step]),
            marks,
            weights,
            found_mine[:5],
        )
        kept = found_other[:5]
        next_grads(found_other[5])
        backs.append((found_mine[5], found_other[5]))
        if step:
            terms = [backs[step][0], pair(backs[step][1])] + ([] if step == 1 else [carry])
            total = added(*terms).astype(BF16)
            carry = ring(total)
        if step + 1 < chips:
            mine = tie(following, found_other[5])
    act_all, pre_all, part_all, rows_all, outs = kept
    rows_all, act_all = tie(rows_all, total), tie(act_all, total)
    grad_widen = dot_tn(rows_all, pre_all).astype(BF16)
    grad_narrow = dot_tn(act_all, part_all).astype(BF16)
    grad_all = added(backs[0][0], pair(backs[0][1]), tie(carry, grad_widen, grad_narrow))
    outs = tie(outs, grad_all)
    grad_hidden = grad_all[:rows]
    table = grad_all[rows : rows + 4 * expert_count, :rows]
    table = jnp.sum(table.reshape(2, expert_count, 2, rows), axis=(0, 2))
    return outs, table, grad_hidden, grad_widen, grad_narrow


def slot_layout(routes, expert_count):
    flat = routes.reshape(-1)
    table = (flat[:, None] == jnp.arange(expert_count, dtype=jnp.int32)[None, :]).astype(jnp.int32)
    before = jnp.cumsum(table, axis=0) - table
    return (flat, jnp.sum(before * table, axis=1))


def to_experts(buffer):
    doubled = jnp.repeat(buffer, 2, axis=0)
    return lax.all_to_all(doubled, "expert", split_axis=0, concat_axis=0, tiled=True)


def both_halves(received, expert_ids, slot_ids):
    slices, capacity, width = received.shape
    summed = jnp.sum(received.astype(F32).reshape(slices // 2, 2, capacity, width), axis=1)
    return summed[expert_ids, slot_ids]


def experts_by_slots(hidden_two, cotangent, routes, gates_table, widen_low, narrow_low, capacity):
    expert_count = gates_table.shape[0]
    device_count = lax.axis_size("expert")
    rows_dev, width = hidden_two.shape
    chooser = (
        routes[:, :, None] == jnp.arange(expert_count, dtype=jnp.int32)[None, None, :]
    ).astype(F32)
    gates = jnp.sum(chooser * gates_table.T[:, None, :], axis=-1)
    expert_ids, slot_ids = slot_layout(routes, expert_count)
    dispatch = (
        jnp.zeros((expert_count, capacity, width), BF16)
        .at[expert_ids, slot_ids]
        .set(jnp.repeat(hidden_two, 2, axis=0))
    )
    expert_rows = to_experts(dispatch).reshape(device_count * capacity, width)
    before_act = dot_nn(expert_rows, widen_low)
    act_low = exact_gelu(before_act).astype(BF16)
    parts_low = dot_nn(act_low, narrow_low).astype(BF16).reshape(device_count, capacity, width)
    returned = lax.all_to_all(parts_low, "expert", split_axis=0, concat_axis=0, tiled=True)
    combined = both_halves(returned, expert_ids, slot_ids).reshape(rows_dev, 2, width)
    out = jnp.sum(gates[:, :, None] * combined, axis=1)
    grad_output = cotangent.astype(F32)
    grad_parts = (
        (gates[:, :, None] * grad_output[:, None, :]).astype(BF16).reshape(2 * rows_dev, width)
    )
    grad_dispatch = (
        jnp.zeros((expert_count, capacity, width), BF16).at[expert_ids, slot_ids].set(grad_parts)
    )
    grad_rows = to_experts(grad_dispatch).reshape(device_count * capacity, width)
    grad_act = dot_nt(grad_rows, narrow_low)
    grad_before = jax.vjp(exact_gelu, before_act)[1](grad_act)[0].astype(BF16)
    grad_narrow = dot_tn(act_low, grad_rows).astype(BF16)
    grad_widen = dot_tn(expert_rows, grad_before).astype(BF16)
    grad_back = dot_nt(grad_before, widen_low).reshape(device_count, capacity, width)
    grad_returned = lax.all_to_all(
        grad_back.astype(BF16), "expert", split_axis=0, concat_axis=0, tiled=True
    )
    grad_hidden = jnp.sum(
        both_halves(grad_returned, expert_ids, slot_ids).reshape(rows_dev, 2, width), axis=1
    )
    grad_gates = jnp.sum(grad_output[:, None, :] * combined, axis=-1)
    table = jnp.sum(grad_gates[:, :, None] * chooser, axis=1).T
    return out, table, grad_hidden, grad_widen, grad_narrow


def local(
    tokens,
    cotangent,
    routes,
    attention_weight,
    attention_first,
    attention_second,
    router_weight,
    router_first,
    router_second,
    norm_vectors,
    norm_first,
    norm_second,
    widen_weight,
    widen_first,
    widen_second,
    narrow_weight,
    narrow_first,
    narrow_second,
):
    device_count = lax.axis_size("expert")
    replicas = lax.axis_size("dp")
    expert_count = device_count // 2
    rows_dev, width = tokens.shape
    capacity = min(rows_dev, 4 * rows_dev // expert_count)
    by_ring = capacity == rows_dev and replicas == 4
    device = lax.axis_index("expert")

    attention_cast = attention_weight.astype(BF16)
    small_own = jnp.concatenate(
        [router_weight.astype(BF16).T, norm_vectors.astype(BF16)], axis=0
    )
    triple_weight = lax.all_gather(attention_cast[:, : 3 * width], "expert", axis=0, tiled=True)
    small_low = gather_expert(small_own, by_ring).transpose(1, 0, 2).reshape(-1, width)
    proj_weight = lax.all_gather(attention_cast[:, 3 * width :], "expert", axis=0, tiled=True)
    router_low = small_low[:expert_count]
    norm_float = small_low[expert_count:].astype(F32)

    widen_cast, narrow_cast = widen_weight[0].astype(BF16), narrow_weight[0].astype(BF16)
    if by_ring:
        half = widen_cast.shape[1] // 2
        halves = jnp.concatenate(
            [widen_cast[:, :half], widen_cast[:, half:], narrow_cast], axis=0
        )
        experts_near, experts_far = gather_dp_near(halves)
    else:
        widen_low = lax.all_gather(widen_cast, "dp", axis=0, tiled=True)
        narrow_low = lax.all_gather(narrow_cast, "dp", axis=0, tiled=True)

    grads_mine = [cotangent]

    def next_grads(dependency):
        if by_ring and len(grads_mine) < expert_count:
            grads_mine.append(ring(tie(grads_mine[-1], dependency)))

    if by_ring and expert_count > 1:
        grads_mine.append(ring(cotangent))
    next_grads(triple_weight)

    below = lax.ppermute(
        tokens[rows_dev - HALO :], "expert", [(i, i + 1) for i in range(device_count - 1)]
    )
    above = lax.ppermute(
        tokens[:HALO], "expert", [(i + 1, i) for i in range(device_count - 1)]
    )
    hidden_one = first_norm(below, tokens, above, norm_float[:2])
    triple = dot_nn(hidden_one, triple_weight).astype(BF16)
    first_row = device * rows_dev
    query_rows = first_row + jnp.arange(rows_dev, dtype=jnp.int32)
    key_rows = first_row - HALO + jnp.arange(rows_dev + 2 * HALO, dtype=jnp.int32)
    query_image = query_rows // SEQ
    inside = (key_rows >= 0) & (key_rows < rows_dev * device_count)
    key_image = jnp.where(inside, key_rows // SEQ, -1)
    heads_low = attention(triple, query_image, key_image)
    next_grads(heads_low)
    if by_ring:
        expert_weights = gather_dp_far(experts_near, experts_far)
    tokens_float = tokens.astype(F32)
    resid = tokens_float + dot_nn(heads_low, proj_weight)
    unit_two, inverse_two = standardised(resid)
    hidden_two = (unit_two * norm_float[2] + norm_float[3]).astype(BF16)

    logits = lax.dot_general(
        router_low, hidden_two, (((1,), (1,)), ((), ())), preferred_element_type=F32
    )
    experts = jnp.arange(expert_count, dtype=jnp.int32)[:, None]
    named = (routes[:, 0][None, :] == experts) | (routes[:, 1][None, :] == experts)
    peak = jnp.max(jnp.where(named, logits, -jnp.inf), axis=0, keepdims=True)
    raised = jnp.where(named, jnp.exp(jnp.where(named, logits - peak, 0.0)), 0.0)
    gates = raised / jnp.sum(raised, axis=0, keepdims=True)

    if by_ring:
        out, grad_gates, grad_hidden, grad_widen, grad_narrow = experts_by_ring(
            hidden_two, gates, expert_weights, next_grads, grads_mine
        )
    else:
        out, grad_gates, grad_hidden, grad_widen, grad_narrow = experts_by_slots(
            hidden_two, cotangent, routes, gates, widen_low, narrow_low, capacity
        )
    if by_ring:
        scattered = [
            scatter_dp_start(grad.reshape(replicas, grad.shape[0] // replicas, grad.shape[1]))
            for grad in (grad_widen, grad_narrow)
        ]

    grad_logits = gates * (grad_gates - jnp.sum(gates * grad_gates, axis=0, keepdims=True))
    grad_router = lax.dot_general(
        grad_logits,
        hidden_two.astype(F32),
        (((1,), (0,)), ((), ())),
        precision=HIGHEST,
        preferred_element_type=F32,
    )
    grad_hidden = grad_hidden + lax.dot_general(
        grad_logits,
        router_low.astype(F32),
        (((0,), (0,)), ((), ())),
        precision=HIGHEST,
        preferred_element_type=F32,
    )
    grad_gain_two = jnp.sum(grad_hidden * unit_two, axis=0)
    grad_shift_two = jnp.sum(grad_hidden, axis=0)
    grad_resid = cotangent.astype(F32) + norm_pull(
        grad_hidden, unit_two, inverse_two, norm_float[2]
    )
    grad_branch = grad_resid.astype(BF16)
    grad_heads = dot_nt(grad_branch, proj_weight).astype(BF16)
    grad_proj = dot_tn(heads_low, grad_branch).astype(BF16)

    grad_triple = attention_back(triple, grad_heads, query_image, key_image)
    by_owner = (2, replicas, expert_count, width // (device_count * replicas))
    small_rows = jnp.concatenate(
        [
            jnp.zeros((2, width), F32),
            jnp.stack([grad_gain_two, grad_shift_two]),
            grad_router,
        ],
        axis=0,
    )
    if by_ring:
        grad_dense, grad_hidden_one = dense_back(
            hidden_one,
            below,
            tokens,
            above,
            grad_triple,
            triple_weight,
            small_rows,
            by_owner,
        )
        dense_sum, (over_pair, over_dp, owned) = sum_to_owner(grad_dense)
        cut = grad_proj.reshape(expert_count, 2, replicas, -1, width).transpose(1, 2, 0, 3, 4)
        proj_sum, _ = sum_to_owner(cut, (grad_heads, grad_triple, over_pair, owned))
        scattered = [scatter_dp_middle(state, over_pair) for state in scattered]
        widen_sum, narrow_sum = [scatter_dp_end(state, over_dp) for state in scattered]
        attention_sum = jnp.concatenate([dense_sum[:, : 3 * width], proj_sum], axis=1)
        small_sum = dense_sum[:, 3 * width :]
    else:
        grad_hidden_one = dot_nt(grad_triple, triple_weight)
        extended = jnp.concatenate([below, tokens, above], axis=0).astype(F32)
        unit_one, _ = standardised(extended)
        small_rows = small_rows.at[0].set(jnp.sum(grad_hidden_one * unit_one, axis=0))
        small_rows = small_rows.at[1].set(jnp.sum(grad_hidden_one, axis=0))
        grad_hidden_one = grad_hidden_one.astype(BF16)
        grad_dense = jnp.concatenate(
            [dot_tn(hidden_one, grad_triple).astype(BF16), grad_proj, small_rows.T.astype(BF16)],
            axis=1,
        )
        widen_sum = lax.psum_scatter(
            grad_widen, "dp", scatter_dimension=0, tiled=True
        ).astype(F32)
        narrow_sum = lax.psum_scatter(
            grad_narrow, "dp", scatter_dimension=0, tiled=True
        ).astype(F32)
        dense_sum = lax.psum(
            lax.psum_scatter(grad_dense, "expert", scatter_dimension=0, tiled=True), "dp"
        ).astype(F32)
        attention_sum = dense_sum[:, : 4 * width]
        small_sum = dense_sum[:, 4 * width :]
    from_above = lax.ppermute(
        grad_hidden_one[:HALO], "expert", [(i + 1, i) for i in range(device_count - 1)]
    )
    from_below = lax.ppermute(
        grad_hidden_one[rows_dev + HALO :],
        "expert",
        [(i, i + 1) for i in range(device_count - 1)],
    )
    if by_ring:
        from_above = tie(from_above, over_dp)
    grad_own = added(
        grad_hidden_one[HALO : HALO + rows_dev],
        jnp.concatenate([from_below, from_above], axis=0),
    )
    unit_one, inverse_one = standardised(tokens_float)
    tokens_grad = grad_resid + norm_pull(grad_own, unit_one, inverse_one, norm_float[0])

    if by_ring:
        out = lax.psum_scatter(out, "expert", scatter_dimension=0, tiled=True)
        out = tie(out, owned).astype(F32)
    mixed = (resid + out).astype(BF16)
    attention_new = adam_step(
        attention_weight, attention_first, attention_second, attention_sum, MATRIX_RATE, DECAY
    )
    if by_ring:
        small_new = small_adam(
            small_sum,
            norm_vectors,
            norm_first,
            norm_second,
            router_weight,
            router_first,
            router_second,
        )
        norm_new, router_new = tuple(small_new[:3]), tuple(small_new[3:])
    else:
        norm_new = adam_step(
            norm_vectors, norm_first, norm_second, small_sum[:, :4].T, VECTOR_RATE, 0.0
        )
        router_new = adam_step(
            router_weight, router_first, router_second, small_sum[:, 4:], MATRIX_RATE, DECAY
        )
    widen_new = adam_step(
        widen_weight, widen_first, widen_second, widen_sum[None], MATRIX_RATE, DECAY
    )
    narrow_new = adam_step(
        narrow_weight, narrow_first, narrow_second, narrow_sum[None], MATRIX_RATE, DECAY
    )
    return (mixed, tokens_grad) + attention_new + router_new + norm_new + widen_new + narrow_new


def solution(mesh):
    rows = P(("dp", "expert"), None)
    dense = P("expert", None)
    vectors = P(None, "expert")
    halves = P("expert", "dp", None)
    return jax.shard_map(
        local,
        mesh=mesh,
        in_specs=(rows,) * 3 + (dense,) * 6 + (vectors,) * 3 + (halves,) * 6,
        out_specs=(rows,) * 2 + (dense,) * 6 + (vectors,) * 3 + (halves,) * 6,
        check_vma=False,
    )
```

```python
import functools

import jax
import jax.numpy as jnp
from jax import lax
from jax.experimental import pallas as pl
from jax.experimental.pallas import tpu as pltpu
from jax.sharding import PartitionSpec as P

HEADS = 12
HEAD_DIM = 64
SEQ = 197
STEP = 5

HIGHEST = lax.Precision.HIGHEST
NORM_EPS = 1e-06
SCORE_SCALE = 0.125
MASKED = -1000000000.0
BETA_ONE = 0.9
BETA_TWO = 0.999
ADAM_EPS = 1e-08
MATRIX_RATE = 0.04
VECTOR_RATE = 0.2
DECAY = 0.1

F32 = jnp.float32
BF16 = jnp.bfloat16
LANES = 128
HALO = 256
QUERY_TILE = 128
KEY_WINDOW = -(-(2 * SEQ + 15) // 16) * 16
ROW_TILE = 256
VMEM_LIMIT = 56 * 1024 * 1024
EARLY = 8
EXTRA = 16
EXPERT_VMEM = 60 * 1024 * 1024


def cheap(flops, bytes_accessed, transcendentals):
    return pl.CostEstimate(
        flops=flops // EARLY,
        bytes_accessed=bytes_accessed // EARLY,
        transcendentals=transcendentals // EARLY,
    )


def tie_kernel(*refs):
    pass


def tie(block, *dependencies):
    anywhere = pl.BlockSpec(memory_space=pl.ANY)
    return pl.pallas_call(
        tie_kernel,
        out_shape=jax.ShapeDtypeStruct(block.shape, block.dtype),
        in_specs=[anywhere] * (1 + len(dependencies)),
        out_specs=anywhere,
        input_output_aliases={0: 0},
        name="tie",
    )(block, *dependencies)


def hop(block, distance):
    count = lax.axis_size("expert")
    return lax.ppermute(block, "expert", [(i, (i + distance) % count) for i in range(count)])


def ring(block):
    return hop(block, 2)


def pair(block):
    return lax.ppermute(block, "expert", [(i, i ^ 1) for i in range(lax.axis_size("expert"))])


def across(block, bit):
    return lax.ppermute(block, "dp", [(i, i ^ bit) for i in range(lax.axis_size("dp"))])


def place_kernel(index, block, *refs):
    refs[-1][0] = block[...]


def place(out, count, block, index):
    anywhere = [pl.BlockSpec(memory_space=pl.ANY)]
    half = (block.shape[0] // 2,) + block.shape[1:]
    return pl.pallas_call(
        place_kernel,
        grid_spec=pltpu.PrefetchScalarGridSpec(
            num_scalar_prefetch=1,
            grid=(2,),
            in_specs=[pl.BlockSpec(half, lambda i, t: (i, 0))] + ([] if out is None else anywhere),
            out_specs=pl.BlockSpec((1,) + half, lambda i, t: (t[0], i, 0)),
        ),
        out_shape=jax.ShapeDtypeStruct((count,) + block.shape, block.dtype),
        input_output_aliases={} if out is None else {2: 0},
        cost_estimate=cheap(
            flops=0, bytes_accessed=2 * block.size * block.dtype.itemsize, transcendentals=0
        ),
        name="place",
    )(*((index.reshape(1), block) + (() if out is None else (out,))))


def gather_dp_near(block):
    count = lax.axis_size("dp")
    if count != 4:
        return lax.all_gather(block, "dp", axis=0), None
    me = lax.axis_index("dp")
    out = place(None, count, block, me)
    for bits in (1, 2):
        out = place(out, count, across(block, bits), me ^ bits)
    return out, across(block, 3)


def gather_dp_far(out, far):
    return out if far is None else place(out, out.shape[0], far, lax.axis_index("dp") ^ 3)


def added(*parts):
    total = parts[0].astype(F32)
    for part in parts[1:]:
        total = total + part.astype(F32)
    return total


def scatter_dp_start(parts):
    one, two = lax.axis_index("dp") % 2, lax.axis_index("dp") // 2
    half = parts.shape[1] // 2
    grid = parts.reshape((2, 2) + parts.shape[1:])
    first, second = grid[:, :, :half], grid[:, :, half:]
    first_got = across(lax.dynamic_index_in_dim(first, 1 - one, 1, False), 1)
    second_got = across(lax.dynamic_index_in_dim(second, 1 - two, 0, False), 2)
    return first, second, first_got, second_got


def scatter_dp_middle(state, then=None):
    one, two = lax.axis_index("dp") % 2, lax.axis_index("dp") // 2
    first, second, first_got, second_got = state
    if then is not None:
        first_got, second_got = tie(first_got, then), tie(second_got, then)
    first_sum = added(lax.dynamic_index_in_dim(first, one, 1, False), first_got).astype(BF16)
    second_sum = added(lax.dynamic_index_in_dim(second, two, 0, False), second_got).astype(BF16)
    first_got = across(lax.dynamic_index_in_dim(first_sum, 1 - two, 0, False), 2)
    second_got = across(lax.dynamic_index_in_dim(second_sum, 1 - one, 0, False), 1)
    return first_sum, second_sum, first_got, second_got


def scatter_dp_end(state, then=None):
    one, two = lax.axis_index("dp") % 2, lax.axis_index("dp") // 2
    first_sum, second_sum, first_got, second_got = state
    if then is not None:
        first_got, second_got = tie(first_got, then), tie(second_got, then)
    first_sum = added(lax.dynamic_index_in_dim(first_sum, two, 0, False), first_got)
    second_sum = added(lax.dynamic_index_in_dim(second_sum, one, 0, False), second_got)
    return jnp.concatenate([first_sum, second_sum], axis=0)


def gather_expert(block, by_hops):
    count = lax.axis_size("expert")
    if not by_hops:
        return lax.all_gather(block, "expert", axis=0)
    chip, core = lax.axis_index("expert") // 2, lax.axis_index("expert") % 2
    given = pair(block)
    both = jnp.where(core == 0, jnp.stack([block, given]), jnp.stack([given, block]))
    blocks = [both] + [hop(both, 2 * step) for step in range(1, count // 2)]
    pieces = []
    for place in range(count // 2):
        piece = blocks[0]
        for step in range(1, count // 2):
            piece = jnp.where((place + step) % (count // 2) == chip, blocks[step], piece)
        pieces.append(piece)
    return jnp.concatenate(pieces, axis=0)


def sum_over_chips(parts):
    chips = parts.shape[0]
    chip = lax.axis_index("expert") // 2
    got = [
        hop(lax.dynamic_index_in_dim(parts, (chip + step) % chips, 0, False), 2 * step)
        for step in range(1, chips)
    ]
    return added(lax.dynamic_index_in_dim(parts, chip, 0, False), *got).astype(BF16)


def spread_over_dp(owned):
    replicas, me = lax.axis_size("dp"), lax.axis_index("dp")
    blocks = [owned] + [across(owned, bits) for bits in range(1, replicas)]
    pieces = []
    for place_at in range(replicas):
        piece = blocks[0]
        for bits in range(1, replicas):
            piece = jnp.where(place_at ^ bits == me, blocks[bits], piece)
        pieces.append(piece.astype(F32))
    return jnp.concatenate(pieces, axis=0)


def standardised(values):
    center = values - jnp.mean(values, axis=-1, keepdims=True)
    spread = jnp.mean(center * center, axis=-1, keepdims=True)
    inverse = lax.rsqrt(spread + NORM_EPS)
    return center * inverse, inverse


def norm_pull(grad, unit, inverse, gain):
    scaled = grad * gain
    mean = jnp.mean(scaled, axis=-1, keepdims=True)
    along = jnp.mean(scaled * unit, axis=-1, keepdims=True)
    return inverse * (scaled - mean - unit * along)


def exact_gelu(values):
    return jax.nn.gelu(values, approximate=False)


def adam_step(weight, first, second, grad, rate, decay):
    new_first = BETA_ONE * first + (1.0 - BETA_ONE) * grad
    new_second = BETA_TWO * second + (1.0 - BETA_TWO) * grad * grad
    mean_hat = new_first / (1.0 - BETA_ONE**STEP)
    square_hat = new_second / (1.0 - BETA_TWO**STEP)
    updated = weight - rate * (mean_hat / (jnp.sqrt(square_hat) + ADAM_EPS) + decay * weight)
    return (new_first, new_second, updated)


def dot_nt(left, right):
    return lax.dot_general(left, right, (((1,), (1,)), ((), ())), preferred_element_type=F32)


def dot_tn(left, right):
    return lax.dot_general(left, right, (((0,), (0,)), ((), ())), preferred_element_type=F32)


def dot_nn(left, right):
    return jnp.dot(left, right, preferred_element_type=F32)


def by_head(block):
    first = lax.broadcasted_iota(jnp.int32, (1, LANES), 1) < HEAD_DIM
    return jnp.concatenate(
        [jnp.where(first, block, 0).astype(BF16), jnp.where(first, 0, block).astype(BF16)], axis=0
    )


def from_heads(turned):
    rows = turned.shape[1] // 2
    return jnp.concatenate([turned[:HEAD_DIM, :rows], turned[HEAD_DIM:, rows:]], axis=0).T


def window_of(starts, tile):
    return pl.ds(pl.multiple_of(starts[tile], 16), KEY_WINDOW)


def attend_tile(tile, window, query_image, key_image, q_ref, keys):
    low = tile * QUERY_TILE
    queries = by_head(q_ref[HALO + low : HALO + low + QUERY_TILE, :] * SCORE_SCALE)
    allowed = key_image[window, :] == query_image[:, low : low + QUERY_TILE]
    allowed = jnp.concatenate([allowed, allowed], axis=1)
    scores = jnp.where(allowed, dot_nt(keys, queries), MASKED)
    raised = jnp.exp(scores - jnp.max(scores, axis=0, keepdims=True))
    return queries, raised * (1.0 / jnp.sum(raised, axis=0, keepdims=True))


def attend_kernel(starts, query_image, key_image, q_ref, k_ref, v_ref, out_ref):
    for tile in range(out_ref.shape[0] // QUERY_TILE):
        window = window_of(starts, tile)
        _, attend = attend_tile(tile, window, query_image, key_image, q_ref, k_ref[window, :])
        found = dot_tn(v_ref[window, :], attend.astype(BF16))
        out_ref[tile * QUERY_TILE : (tile + 1) * QUERY_TILE, :] = from_heads(found).astype(BF16)


def image_specs(span, rows, blocks):
    return [
        pl.BlockSpec((1, rows), lambda i, t: (0, 0)),
        pl.BlockSpec((span, 1), lambda i, t: (0, 0)),
        pl.BlockSpec((span, LANES), lambda i, t: (0, i)),
        pl.BlockSpec((span, LANES), lambda i, t: (0, blocks + i)),
        pl.BlockSpec((span, LANES), lambda i, t: (0, 2 * blocks + i)),
    ]


def attention(triple, starts, query_image, key_image):
    span = triple.shape[0]
    rows = span - 2 * HALO
    width = triple.shape[1] // 3
    blocks = width // LANES
    cost = HEADS * rows * KEY_WINDOW
    return pl.pallas_call(
        attend_kernel,
        grid_spec=pltpu.PrefetchScalarGridSpec(
            num_scalar_prefetch=1,
            grid=(blocks,),
            in_specs=image_specs(span, rows, blocks),
            out_specs=pl.BlockSpec((rows, LANES), lambda i, t: (0, i)),
        ),
        out_shape=jax.ShapeDtypeStruct((rows, width), BF16),
        compiler_params=pltpu.CompilerParams(vmem_limit_bytes=VMEM_LIMIT),
        cost_estimate=cheap(
            flops=cost * 512, bytes_accessed=span * width * 6, transcendentals=cost
        ),
        name="attention",
    )(starts, query_image[None, :], key_image[:, None], triple, triple, triple)


def attend_back_kernel(
    starts, query_image, key_image, q_ref, k_ref, v_ref, g_ref, out_ref, dk, dv
):
    rows = g_ref.shape[0]
    span = k_ref.shape[0]
    width = out_ref.shape[1] // 3
    column = pl.program_id(0) * LANES

    def columns(part):
        return pl.ds(pl.multiple_of(part * width + column, LANES), LANES)

    dk[...] = jnp.zeros_like(dk)
    dv[...] = jnp.zeros_like(dv)
    out_ref[:HALO, columns(0)] = jnp.zeros((HALO, LANES), BF16)
    out_ref[span - HALO :, columns(0)] = jnp.zeros((HALO, LANES), BF16)
    for tile in range(rows // QUERY_TILE):
        low = tile * QUERY_TILE
        window = window_of(starts, tile)
        keys = k_ref[window, :]
        queries, attend = attend_tile(tile, window, query_image, key_image, q_ref, keys)
        grads = by_head(g_ref[low : low + QUERY_TILE, :])
        pulled = dot_nt(v_ref[window, :], grads)
        inner = jnp.sum(attend * pulled, axis=0, keepdims=True)
        score_grad = (attend * (pulled - inner)).astype(BF16)
        dv[window, :] += dot_nn(attend.astype(BF16), grads)
        dk[window, :] += dot_nn(score_grad, queries)
        query_grad = from_heads(dot_tn(keys, score_grad)) * SCORE_SCALE
        out_ref[HALO + low : HALO + low + QUERY_TILE, columns(0)] = query_grad.astype(BF16)
    out_ref[:, columns(1)] = dk[...].astype(BF16)
    out_ref[:, columns(2)] = dv[...].astype(BF16)


def attention_back(triple, grads, starts, query_image, key_image):
    span = triple.shape[0]
    rows = span - 2 * HALO
    width = triple.shape[1] // 3
    blocks = width // LANES
    cost = HEADS * rows * KEY_WINDOW
    return pl.pallas_call(
        attend_back_kernel,
        grid_spec=pltpu.PrefetchScalarGridSpec(
            num_scalar_prefetch=1,
            grid=(blocks,),
            in_specs=image_specs(span, rows, blocks)
            + [pl.BlockSpec((rows, LANES), lambda i, t: (0, i))],
            out_specs=pl.BlockSpec((span, 3 * width), lambda i, t: (0, 0)),
            scratch_shapes=[pltpu.VMEM((span, LANES), F32), pltpu.VMEM((span, LANES), F32)],
        ),
        out_shape=jax.ShapeDtypeStruct((span, 3 * width), BF16),
        compiler_params=pltpu.CompilerParams(vmem_limit_bytes=VMEM_LIMIT),
        cost_estimate=cheap(
            flops=cost * 1280, bytes_accessed=span * width * 14, transcendentals=cost
        ),
        name="attention_back",
    )(starts, query_image[None, :], key_image[:, None], triple, triple, triple, grads)


def first_norm_kernel(below, tokens, above, vectors, out):
    low = 0
    for block in (below, tokens, above):
        unit, _ = standardised(block[...].astype(F32))
        out[low : low + block.shape[0], :] = (unit * vectors[0:1] + vectors[1:2]).astype(BF16)
        low += block.shape[0]


def first_norm(below, tokens, above, vectors):
    span, width = tokens.shape[0] + 2 * HALO, tokens.shape[1]
    return pl.pallas_call(
        first_norm_kernel,
        out_shape=jax.ShapeDtypeStruct((span, width), BF16),
        compiler_params=pltpu.CompilerParams(vmem_limit_bytes=VMEM_LIMIT),
        cost_estimate=cheap(
            flops=span * width * 10, bytes_accessed=span * width * 4, transcendentals=0
        ),
        name="first_norm",
    )(below, tokens, above, vectors)


def dense_back_kernel(
    layout,
    me,
    hidden,
    below,
    tokens,
    above,
    grads,
    weight,
    heads,
    branch,
    small,
    give_out,
    keep_out,
    back_out,
):
    cores, replicas, chips, rows = layout
    width = hidden.shape[1]
    gain = jnp.zeros((1, width), F32)
    shift = jnp.zeros((1, width), F32)
    low = 0
    for block in (below, tokens, above):
        here = slice(low, low + block.shape[0])
        back = dot_nt(grads[here, :], weight[...])
        back_out[here, :] = back.astype(BF16)
        unit, _ = standardised(block[...].astype(F32))
        gain += jnp.sum(back * unit, axis=0, keepdims=True)
        shift += jnp.sum(back, axis=0, keepdims=True)
        low += block.shape[0]
    sums = jnp.concatenate(
        [
            gain,
            shift,
            jnp.zeros((6, width), F32),
        ],
        axis=0,
    )
    lane = lax.broadcasted_iota(jnp.int32, (8, LANES), 1)
    row = lax.broadcasted_iota(jnp.int32, (8, LANES), 0)
    spread = (lane == row).astype(F32)

    def store(low, block):
        for core in range(cores):

            def put(out, core=core):
                for chip in range(chips):
                    for replica in range(replicas):
                        start = ((chip * cores + core) * replicas + replica) * rows
                        piece = block[start : start + rows].astype(BF16)
                        out[replica, chip, :, low : low + block.shape[1]] = piece

            pl.when(me[0] == core)(lambda: put(keep_out))
            pl.when(me[0] != core)(lambda: put(give_out))

    for low in range(0, 3 * width, width):
        store(low, dot_tn(hidden[...], grads[:, low : low + width]))
    store(3 * width, dot_tn(heads[...], branch[...]))
    store(
        4 * width,
        lax.dot_general(
            small[...] + sums,
            spread,
            (((0,), (0,)), ((), ())),
            precision=HIGHEST,
            preferred_element_type=F32,
        ),
    )


def dense_back(hidden, below, tokens, above, grads, weight, heads, branch, small, layout):
    span, width = hidden.shape
    columns = 4 * width + LANES
    core = lax.axis_index("expert") % 2
    return pl.pallas_call(
        functools.partial(dense_back_kernel, layout),
        out_shape=[
            jax.ShapeDtypeStruct(layout[1:] + (columns,), BF16),
            jax.ShapeDtypeStruct(layout[1:] + (columns,), BF16),
            jax.ShapeDtypeStruct((span, width), BF16),
        ],
        in_specs=[pl.BlockSpec(memory_space=pltpu.SMEM)]
        + [pl.BlockSpec(memory_space=pltpu.VMEM)] * 9,
        compiler_params=pltpu.CompilerParams(vmem_limit_bytes=VMEM_LIMIT),
        cost_estimate=cheap(
            flops=span * width * width * 12,
            bytes_accessed=span * width * 16 + width * width * 12,
            transcendentals=0,
        ),
        name="dense_back",
    )(core.reshape(1), hidden, below, tokens, above, grads, weight, heads, branch, small)


def small_adam_kernel(sums, *refs):
    values = [ref[...] for ref in refs[:6]]
    vectors, matrix = refs[0].shape[0], refs[3].shape[0]
    rows = sums.shape[0]
    lane = lax.broadcasted_iota(jnp.int32, (rows, rows), 1)
    row = lax.broadcasted_iota(jnp.int32, (rows, rows), 0)
    turned = lax.dot_general(
        sums[...],
        (lane == row).astype(F32),
        (((0,), (0,)), ((), ())),
        precision=HIGHEST,
        preferred_element_type=F32,
    )
    found = adam_step(*values[:3], turned[:vectors], VECTOR_RATE, 0.0)
    found += adam_step(*values[3:], turned[vectors : vectors + matrix], MATRIX_RATE, DECAY)
    for ref, value in zip(refs[6:], found):
        ref[...] = value


def small_adam(sums, *arrays):
    return pl.pallas_call(
        small_adam_kernel,
        out_shape=[jax.ShapeDtypeStruct(array.shape, F32) for array in arrays],
        name="small_adam",
    )(sums, *arrays)


def gelu_and_slope(values):
    inverse = 1.0 / (1.0 + (0.3275911 * 0.7071067811865476) * jnp.abs(values))
    fit = 1.061405429 * inverse - 1.453152027
    fit = fit * inverse + 1.421413741
    fit = fit * inverse - 0.284496736
    fit = fit * inverse + 0.254829592
    bell = jnp.exp(-0.5 * values * values)
    tail = (0.5 * fit) * (inverse * bell)
    share = jnp.where(values >= 0.0, 1.0 - tail, tail)
    return values * share, share + values * (bell * 0.3989422804014327)


def expert_kernel(first, target, rows_ref, grads_ref, gates, mark, place, weights, *refs):
    outs = refs if first else refs[5:]
    act_out, pre_out, part_out, rows_out, mixed_out, back_out = outs
    tile = pl.program_id(0)
    rows = rows_ref[...]
    gate = dot_tn(gates[...], mark[...])
    width = rows.shape[1]
    gate = jnp.concatenate([gate] * (width // LANES), axis=1)
    grads_float = grads_ref[...].astype(F32)
    grad_part = (gate * grads_float).astype(BF16)
    rows_out[...] = rows
    part_out[...] = grad_part
    part = None
    back = None
    replicas, parts, size = weights.shape
    quarter = parts // 4
    narrow_all = weights[:, 2 * quarter :, :].reshape(2 * size, width)
    for turn in range(2):
        here = slice(turn * size, (turn + 1) * size)
        widen = weights[:, turn * quarter : (turn + 1) * quarter, :].reshape(width, size)
        narrow = narrow_all[here, :]
        before = dot_nn(rows, widen)
        pulled = dot_nt(grad_part, narrow)
        act, slope = gelu_and_slope(before)
        act = act.astype(BF16)
        grad_pre = (pulled * slope).astype(BF16)
        act_out[:, here] = act
        pre_out[:, here] = grad_pre
        part_here = dot_nn(act, narrow)
        back_here = dot_nt(grad_pre, widen)
        part = part_here if part is None else part + part_here
        back = back_here if back is None else back + back_here
    part = part.astype(BF16).astype(F32)
    product = part * grads_float
    folded = product[:, :LANES]
    for low in range(LANES, width, LANES):
        folded = folded + product[:, low : low + LANES]
    dots = lax.dot_general(
        jnp.ones((EXTRA, LANES), F32),
        folded,
        (((1,), (1,)), ((), ())),
        precision=HIGHEST,
        preferred_element_type=F32,
    )
    high = dots.astype(BF16).astype(F32)
    dots = high * place[0] + (dots - high) * place[1]
    mixed_out[...] = (gate * part).astype(BF16)
    count = rows.shape[0]
    back_out[pl.ds(pl.multiple_of(tile * count, count), count), :] = back.astype(BF16)
    extra = slice(back_out.shape[0] - EXTRA, back_out.shape[0])
    back_out[extra, pl.ds(pl.multiple_of(tile * count, count), count)] = dots.astype(BF16)


def expert_block(place, places, target, payload, grads_block, marks, weights, kept):
    rows, width = grads_block.shape
    replicas, parts, _ = weights.shape
    hidden = parts * replicas // 2
    tiles = rows // ROW_TILE
    every = places * rows
    by_tile = pl.BlockSpec((ROW_TILE, width), lambda i, t: (i, 0))
    at = lambda i, t: (place * tiles + i, 0)
    whole = lambda i, t: (0, 0)
    first = kept is None
    kept = () if first else kept
    gate_mark, dot_mark = marks
    return pl.pallas_call(
        functools.partial(expert_kernel, first),
        grid_spec=pltpu.PrefetchScalarGridSpec(
            num_scalar_prefetch=1,
            grid=(tiles,),
            in_specs=[
                by_tile,
                by_tile,
                pl.BlockSpec((EXTRA, ROW_TILE), lambda i, t: (rows // EXTRA, i)),
                pl.BlockSpec((EXTRA, LANES), whole),
                pl.BlockSpec((2, EXTRA, 1), lambda i, t: (0, 0, 0)),
                pl.BlockSpec(
                    (replicas, parts, width), lambda i, t: (0, 0, 0), pipeline_mode=pl.Buffered(1)
                ),
            ]
            + [pl.BlockSpec(memory_space=pl.ANY)] * len(kept),
            out_specs=[
                pl.BlockSpec((ROW_TILE, hidden), at),
                pl.BlockSpec((ROW_TILE, hidden), at),
                pl.BlockSpec((ROW_TILE, width), at),
                pl.BlockSpec((ROW_TILE, width), at),
                pl.BlockSpec((ROW_TILE, width), lambda i, t: (t[0] * tiles + i, 0)),
                pl.BlockSpec((rows + EXTRA, width), whole),
            ],
        ),
        out_shape=[
            pltpu.HBM((every, hidden), BF16),
            pltpu.HBM((every, hidden), BF16),
            pltpu.HBM((every, width), BF16),
            pltpu.HBM((every, width), BF16),
            pltpu.HBM((every, width), BF16),
            jax.ShapeDtypeStruct((rows + EXTRA, width), BF16),
        ],
        input_output_aliases={7 + i: i for i in range(len(kept))},
        compiler_params=pltpu.CompilerParams(vmem_limit_bytes=EXPERT_VMEM),
        cost_estimate=cheap(
            flops=rows * width * hidden * 8,
            bytes_accessed=rows * (2 * hidden + 6 * width) * 2 + 4 * width * hidden,
            transcendentals=rows * hidden,
        ),
        name="expert_block",
    )(
        target.reshape(1),
        payload,
        grads_block,
        payload,
        gate_mark,
        dot_mark,
        weights,
        *kept,
    )


def split_float(values, terms):
    parts = []
    for _ in range(terms):
        part = lax.reduce_precision(values, 8, 7)
        parts.append(part.astype(BF16))
        values = values - part
    return parts


def experts_by_ring(hidden_two, gates, weights, next_grads, grads_mine):
    chips = lax.axis_size("expert") // 2
    expert_count, rows = gates.shape
    width = hidden_two.shape[1]
    chip, core = lax.axis_index("expert") // 2, lax.axis_index("expert") % 2
    number = jnp.arange(EXTRA, dtype=jnp.int32)[:, None]
    gate_mark = jnp.broadcast_to(
        (number % expert_count == chip) & (number < 3 * expert_count), (EXTRA, LANES)
    ).astype(BF16)
    slot = 2 * (core * expert_count + chip)
    dot_mark = jnp.stack([number == slot, number == slot + 1]).astype(F32)
    marks = (gate_mark, dot_mark)
    carried = jnp.pad(
        jnp.concatenate(split_float(gates, 3), axis=0),
        ((0, EXTRA - 3 * expert_count), (0, width - rows)),
    )
    kept = None
    carry = None
    backs = []
    mine = jnp.concatenate([hidden_two, carried], axis=0)
    for step in range(chips):
        other = pair(mine)
        if step + 1 < chips:
            following = ring(mine)
        source = (chip - step) % chips
        found_mine = expert_block(
            2 * step,
            2 * chips,
            2 * source + core,
            mine,
            grads_mine[step],
            marks,
            weights,
            kept,
        )
        found_other = expert_block(
            2 * step + 1,
            2 * chips,
            2 * source + 1 - core,
            other,
            pair(grads_mine[step]),
            marks,
            weights,
            found_mine[:5],
        )
        kept = found_other[:5]
        next_grads(found_other[5])
        backs.append((found_mine[5], found_other[5]))
        if step:
            terms = [backs[step][0], pair(backs[step][1])] + ([] if step == 1 else [carry])
            total = added(*terms).astype(BF16)
            carry = ring(total)
        if step + 1 < chips:
            mine = tie(following, found_other[5], *grads_mine[step + 1 :])
    act_all, pre_all, part_all, rows_all, outs = kept
    rows_all, act_all = tie(rows_all, total), tie(act_all, total)
    grad_widen = dot_tn(rows_all, pre_all).astype(BF16)
    grad_narrow = dot_tn(act_all, part_all).astype(BF16)
    grad_all = added(backs[0][0], pair(backs[0][1]), tie(carry, grad_widen, grad_narrow))
    outs = tie(outs, total)
    grad_hidden = grad_all[:rows]
    table = grad_all[rows : rows + 4 * expert_count, :rows]
    table = jnp.sum(table.reshape(2, expert_count, 2, rows), axis=(0, 2))
    return outs, table, grad_hidden, grad_widen, grad_narrow


def slot_layout(routes, expert_count):
    flat = routes.reshape(-1)
    table = (flat[:, None] == jnp.arange(expert_count, dtype=jnp.int32)[None, :]).astype(jnp.int32)
    before = jnp.cumsum(table, axis=0) - table
    return (flat, jnp.sum(before * table, axis=1))


def to_experts(buffer):
    doubled = jnp.repeat(buffer, 2, axis=0)
    return lax.all_to_all(doubled, "expert", split_axis=0, concat_axis=0, tiled=True)


def both_halves(received, expert_ids, slot_ids):
    slices, capacity, width = received.shape
    summed = jnp.sum(received.astype(F32).reshape(slices // 2, 2, capacity, width), axis=1)
    return summed[expert_ids, slot_ids]


def experts_by_slots(hidden_two, cotangent, routes, gates_table, widen_low, narrow_low, capacity):
    expert_count = gates_table.shape[0]
    device_count = lax.axis_size("expert")
    rows_dev, width = hidden_two.shape
    chooser = (
        routes[:, :, None] == jnp.arange(expert_count, dtype=jnp.int32)[None, None, :]
    ).astype(F32)
    gates = jnp.sum(chooser * gates_table.T[:, None, :], axis=-1)
    expert_ids, slot_ids = slot_layout(routes, expert_count)
    dispatch = (
        jnp.zeros((expert_count, capacity, width), BF16)
        .at[expert_ids, slot_ids]
        .set(jnp.repeat(hidden_two, 2, axis=0))
    )
    expert_rows = to_experts(dispatch).reshape(device_count * capacity, width)
    before_act = dot_nn(expert_rows, widen_low)
    act_low = exact_gelu(before_act).astype(BF16)
    parts_low = dot_nn(act_low, narrow_low).astype(BF16).reshape(device_count, capacity, width)
    returned = lax.all_to_all(parts_low, "expert", split_axis=0, concat_axis=0, tiled=True)
    combined = both_halves(returned, expert_ids, slot_ids).reshape(rows_dev, 2, width)
    out = jnp.sum(gates[:, :, None] * combined, axis=1)
    grad_output = cotangent.astype(F32)
    grad_parts = (
        (gates[:, :, None] * grad_output[:, None, :]).astype(BF16).reshape(2 * rows_dev, width)
    )
    grad_dispatch = (
        jnp.zeros((expert_count, capacity, width), BF16).at[expert_ids, slot_ids].set(grad_parts)
    )
    grad_rows = to_experts(grad_dispatch).reshape(device_count * capacity, width)
    grad_act = dot_nt(grad_rows, narrow_low)
    grad_before = jax.vjp(exact_gelu, before_act)[1](grad_act)[0].astype(BF16)
    grad_narrow = dot_tn(act_low, grad_rows).astype(BF16)
    grad_widen = dot_tn(expert_rows, grad_before).astype(BF16)
    grad_back = dot_nt(grad_before, widen_low).reshape(device_count, capacity, width)
    grad_returned = lax.all_to_all(
        grad_back.astype(BF16), "expert", split_axis=0, concat_axis=0, tiled=True
    )
    grad_hidden = jnp.sum(
        both_halves(grad_returned, expert_ids, slot_ids).reshape(rows_dev, 2, width), axis=1
    )
    grad_gates = jnp.sum(grad_output[:, None, :] * combined, axis=-1)
    table = jnp.sum(grad_gates[:, :, None] * chooser, axis=1).T
    return out, table, grad_hidden, grad_widen, grad_narrow


def local(
    tokens,
    cotangent,
    routes,
    attention_weight,
    attention_first,
    attention_second,
    router_weight,
    router_first,
    router_second,
    norm_vectors,
    norm_first,
    norm_second,
    widen_weight,
    widen_first,
    widen_second,
    narrow_weight,
    narrow_first,
    narrow_second,
):
    device_count = lax.axis_size("expert")
    replicas = lax.axis_size("dp")
    expert_count = device_count // 2
    rows_dev, width = tokens.shape
    capacity = min(rows_dev, 4 * rows_dev // expert_count)
    by_ring = capacity == rows_dev and replicas == 4
    device = lax.axis_index("expert")

    attention_cast = attention_weight.astype(BF16)
    small_own = jnp.concatenate(
        [router_weight.astype(BF16).T, norm_vectors.astype(BF16)], axis=0
    )
    triple_weight = lax.all_gather(attention_cast[:, : 3 * width], "expert", axis=0, tiled=True)
    small_low = gather_expert(small_own, by_ring).transpose(1, 0, 2).reshape(-1, width)
    proj_weight = lax.all_gather(attention_cast[:, 3 * width :], "expert", axis=0, tiled=True)
    router_low = small_low[:expert_count]
    norm_float = small_low[expert_count:].astype(F32)

    widen_cast, narrow_cast = widen_weight[0].astype(BF16), narrow_weight[0].astype(BF16)
    if by_ring:
        half = widen_cast.shape[1] // 2
        halves = jnp.concatenate(
            [widen_cast[:, :half], widen_cast[:, half:], narrow_cast], axis=0
        )
        experts_near, experts_far = gather_dp_near(halves)
    else:
        widen_low = lax.all_gather(widen_cast, "dp", axis=0, tiled=True)
        narrow_low = lax.all_gather(narrow_cast, "dp", axis=0, tiled=True)

    grads_mine = [cotangent]

    def next_grads(*dependencies):
        if by_ring and len(grads_mine) < expert_count:
            grads_mine[-1] = tie(grads_mine[-1], *dependencies)
            grads_mine.append(ring(grads_mine[-1]))

    next_grads(small_low)

    below = lax.ppermute(
        tokens[rows_dev - HALO :], "expert", [(i, i + 1) for i in range(device_count - 1)]
    )
    above = lax.ppermute(
        tokens[:HALO], "expert", [(i + 1, i) for i in range(device_count - 1)]
    )
    if by_ring:
        below = tie(below, experts_near)
    hidden_one = first_norm(below, tokens, above, norm_float[:2])
    next_grads(hidden_one, triple_weight)
    triple = dot_nn(hidden_one, triple_weight).astype(BF16)
    first_row = device * rows_dev
    query_rows = first_row + jnp.arange(rows_dev, dtype=jnp.int32)
    key_rows = first_row - HALO + jnp.arange(rows_dev + 2 * HALO, dtype=jnp.int32)
    query_image = query_rows // SEQ
    inside = (key_rows >= 0) & (key_rows < rows_dev * device_count)
    key_image = jnp.where(inside, key_rows // SEQ, -1)
    tile_rows = first_row + QUERY_TILE * jnp.arange(rows_dev // QUERY_TILE, dtype=jnp.int32)
    starts = tile_rows // SEQ * SEQ - (first_row - HALO)
    starts = jnp.minimum(starts // 16 * 16, rows_dev + 2 * HALO - KEY_WINDOW)
    heads_low = attention(triple, starts, query_image, key_image)
    if by_ring:
        expert_weights = gather_dp_far(experts_near, experts_far)
    tokens_float = tokens.astype(F32)
    resid = tokens_float + dot_nn(heads_low, proj_weight)
    unit_two, inverse_two = standardised(resid)
    hidden_two = (unit_two * norm_float[2] + norm_float[3]).astype(BF16)

    if by_ring:
        hidden_two = tie(hidden_two, grads_mine[-1])
    next_grads(hidden_two)

    logits = lax.dot_general(
        router_low, hidden_two, (((1,), (1,)), ((), ())), preferred_element_type=F32
    )
    experts = jnp.arange(expert_count, dtype=jnp.int32)[:, None]
    named = (routes[:, 0][None, :] == experts) | (routes[:, 1][None, :] == experts)
    peak = jnp.max(jnp.where(named, logits, -jnp.inf), axis=0, keepdims=True)
    raised = jnp.where(named, jnp.exp(jnp.where(named, logits - peak, 0.0)), 0.0)
    gates = raised / jnp.sum(raised, axis=0, keepdims=True)

    if by_ring:
        out, grad_gates, grad_hidden, grad_widen, grad_narrow = experts_by_ring(
            hidden_two, gates, expert_weights, next_grads, grads_mine
        )
    else:
        out, grad_gates, grad_hidden, grad_widen, grad_narrow = experts_by_slots(
            hidden_two, cotangent, routes, gates, widen_low, narrow_low, capacity
        )
    if by_ring:
        scattered = [
            scatter_dp_start(grad.reshape(replicas, grad.shape[0] // replicas, grad.shape[1]))
            for grad in (grad_widen, grad_narrow)
        ]

    grad_logits = gates * (grad_gates - jnp.sum(gates * grad_gates, axis=0, keepdims=True))
    grad_router = lax.dot_general(
        grad_logits,
        hidden_two.astype(F32),
        (((1,), (0,)), ((), ())),
        precision=HIGHEST,
        preferred_element_type=F32,
    )
    grad_hidden = grad_hidden + lax.dot_general(
        grad_logits,
        router_low.astype(F32),
        (((0,), (0,)), ((), ())),
        precision=HIGHEST,
        preferred_element_type=F32,
    )
    grad_gain_two = jnp.sum(grad_hidden * unit_two, axis=0)
    grad_shift_two = jnp.sum(grad_hidden, axis=0)
    grad_resid = cotangent.astype(F32) + norm_pull(
        grad_hidden, unit_two, inverse_two, norm_float[2]
    )
    grad_branch = grad_resid.astype(BF16)
    grad_heads = dot_nt(grad_branch, proj_weight).astype(BF16)

    grad_triple = attention_back(triple, grad_heads, starts, query_image, key_image)
    if by_ring:
        scattered = [scatter_dp_middle(state, grad_triple) for state in scattered]
        grad_triple = tie(grad_triple, *(part for state in scattered for part in state[:2]))
    by_owner = (2, replicas, expert_count, width // (device_count * replicas))
    small_rows = jnp.concatenate(
        [
            jnp.zeros((2, width), F32),
            jnp.stack([grad_gain_two, grad_shift_two]),
            grad_router,
        ],
        axis=0,
    )
    if by_ring:
        grad_give, grad_keep, grad_hidden_one = dense_back(
            hidden_one,
            below,
            tokens,
            above,
            grad_triple,
            triple_weight,
            heads_low,
            grad_branch,
            small_rows,
            by_owner,
        )
        out = lax.psum_scatter(out, "expert", scatter_dimension=0, tiled=True)
        over_pair = added(grad_keep, pair(tie(grad_give, out))).astype(BF16)
        over_dp = scatter_dp_end(scatter_dp_middle(scatter_dp_start(over_pair)))
        over_dp = over_dp.astype(BF16)
        owned = sum_over_chips(over_dp)
        dense_sum = spread_over_dp(owned)
        widen_sum, narrow_sum = [scatter_dp_end(state, over_pair) for state in scattered]
        out = tie(out, owned)
        attention_sum = dense_sum[:, : 4 * width]
        small_sum = dense_sum[:, 4 * width :]
    else:
        grad_hidden_one = dot_nt(grad_triple, triple_weight)
        extended = jnp.concatenate([below, tokens, above], axis=0).astype(F32)
        unit_one, _ = standardised(extended)
        small_rows = small_rows.at[0].set(jnp.sum(grad_hidden_one * unit_one, axis=0))
        small_rows = small_rows.at[1].set(jnp.sum(grad_hidden_one, axis=0))
        grad_hidden_one = grad_hidden_one.astype(BF16)
        grad_dense = jnp.concatenate(
            [
                dot_tn(hidden_one, grad_triple).astype(BF16),
                dot_tn(heads_low, grad_branch).astype(BF16),
                small_rows.T.astype(BF16),
            ],
            axis=1,
        )
        widen_sum = lax.psum_scatter(
            grad_widen, "dp", scatter_dimension=0, tiled=True
        ).astype(F32)
        narrow_sum = lax.psum_scatter(
            grad_narrow, "dp", scatter_dimension=0, tiled=True
        ).astype(F32)
        dense_sum = lax.psum(
            lax.psum_scatter(grad_dense, "expert", scatter_dimension=0, tiled=True), "dp"
        ).astype(F32)
        attention_sum = dense_sum[:, : 4 * width]
        small_sum = dense_sum[:, 4 * width :]
    from_above = lax.ppermute(
        grad_hidden_one[:HALO], "expert", [(i + 1, i) for i in range(device_count - 1)]
    )
    from_below = lax.ppermute(
        grad_hidden_one[rows_dev + HALO :],
        "expert",
        [(i, i + 1) for i in range(device_count - 1)],
    )
    if by_ring:
        from_above = tie(from_above, over_dp)
    grad_own = added(
        grad_hidden_one[HALO : HALO + rows_dev],
        jnp.concatenate([from_below, from_above], axis=0),
    )
    unit_one, inverse_one = standardised(tokens_float)
    tokens_grad = grad_resid + norm_pull(grad_own, unit_one, inverse_one, norm_float[0])

    if by_ring:
        out = out.astype(F32)
    mixed = (resid + out).astype(BF16)
    attention_new = adam_step(
        attention_weight, attention_first, attention_second, attention_sum, MATRIX_RATE, DECAY
    )
    if by_ring:
        small_new = small_adam(
            small_sum,
            norm_vectors,
            norm_first,
            norm_second,
            router_weight.T,
            router_first.T,
            router_second.T,
        )
        norm_new = tuple(small_new[:3])
        router_new = tuple(array.T for array in small_new[3:])
    else:
        norm_new = adam_step(
            norm_vectors, norm_first, norm_second, small_sum[:, :4].T, VECTOR_RATE, 0.0
        )
        router_new = adam_step(
            router_weight, router_first, router_second, small_sum[:, 4:], MATRIX_RATE, DECAY
        )
    widen_new = adam_step(
        widen_weight, widen_first, widen_second, widen_sum[None], MATRIX_RATE, DECAY
    )
    narrow_new = adam_step(
        narrow_weight, narrow_first, narrow_second, narrow_sum[None], MATRIX_RATE, DECAY
    )
    return (mixed, tokens_grad) + attention_new + router_new + norm_new + widen_new + narrow_new


def solution(mesh):
    rows = P(("dp", "expert"), None)
    dense = P("expert", None)
    vectors = P(None, "expert")
    halves = P("expert", "dp", None)
    return jax.shard_map(
        local,
        mesh=mesh,
        in_specs=(rows,) * 3 + (dense,) * 6 + (vectors,) * 3 + (halves,) * 6,
        out_specs=(rows,) * 2 + (dense,) * 6 + (vectors,) * 3 + (halves,) * 6,
        check_vma=False,
    )
```

```python
import functools

import jax
import jax.numpy as jnp
from jax import lax
from jax.experimental import pallas as pl
from jax.experimental.pallas import tpu as pltpu
from jax.sharding import PartitionSpec as P

HEADS = 12
HEAD_DIM = 64
SEQ = 197
STEP = 5

HIGHEST = lax.Precision.HIGHEST
NORM_EPS = 1e-06
SCORE_SCALE = 0.125
MASKED = -1000000000.0
BETA_ONE = 0.9
BETA_TWO = 0.999
ADAM_EPS = 1e-08
MATRIX_RATE = 0.04
VECTOR_RATE = 0.2
DECAY = 0.1

F32 = jnp.float32
BF16 = jnp.bfloat16
LANES = 128
HALO = 256
QUERY_TILE = 128
KEY_WINDOW = -(-(2 * SEQ + 15) // 16) * 16
ROW_TILE = 256
VMEM_LIMIT = 56 * 1024 * 1024
EARLY = 8
EXTRA = 16
EXPERT_VMEM = 60 * 1024 * 1024


def cheap(flops, bytes_accessed, transcendentals):
    return pl.CostEstimate(
        flops=flops // EARLY,
        bytes_accessed=bytes_accessed // EARLY,
        transcendentals=transcendentals // EARLY,
    )


def tie_kernel(*refs):
    pass


def tie(block, *dependencies):
    anywhere = pl.BlockSpec(memory_space=pl.ANY)
    return pl.pallas_call(
        tie_kernel,
        out_shape=jax.ShapeDtypeStruct(block.shape, block.dtype),
        in_specs=[anywhere] * (1 + len(dependencies)),
        out_specs=anywhere,
        input_output_aliases={0: 0},
        name="tie",
    )(block, *dependencies)


def hop(block, distance):
    count = lax.axis_size("expert")
    return lax.ppermute(block, "expert", [(i, (i + distance) % count) for i in range(count)])


def ring(block):
    return hop(block, 2)


def pair(block):
    return lax.ppermute(block, "expert", [(i, i ^ 1) for i in range(lax.axis_size("expert"))])


def across(block, bit):
    return lax.ppermute(block, "dp", [(i, i ^ bit) for i in range(lax.axis_size("dp"))])


def place_kernel(index, block, *refs):
    refs[-1][0] = block[...]


def place(out, count, block, index):
    anywhere = [pl.BlockSpec(memory_space=pl.ANY)]
    half = (block.shape[0] // 2,) + block.shape[1:]
    return pl.pallas_call(
        place_kernel,
        grid_spec=pltpu.PrefetchScalarGridSpec(
            num_scalar_prefetch=1,
            grid=(2,),
            in_specs=[pl.BlockSpec(half, lambda i, t: (i, 0))] + ([] if out is None else anywhere),
            out_specs=pl.BlockSpec((1,) + half, lambda i, t: (t[0], i, 0)),
        ),
        out_shape=jax.ShapeDtypeStruct((count,) + block.shape, block.dtype),
        input_output_aliases={} if out is None else {2: 0},
        cost_estimate=cheap(
            flops=0, bytes_accessed=2 * block.size * block.dtype.itemsize, transcendentals=0
        ),
        name="place",
    )(*((index.reshape(1), block) + (() if out is None else (out,))))


def gather_dp_near(block):
    count = lax.axis_size("dp")
    if count != 4:
        return lax.all_gather(block, "dp", axis=0), None
    me = lax.axis_index("dp")
    out = place(None, count, block, me)
    for bits in (1, 2):
        out = place(out, count, across(block, bits), me ^ bits)
    return out, across(tie(block, out), 3)


def gather_dp_far(out, far):
    return out if far is None else place(out, out.shape[0], far, lax.axis_index("dp") ^ 3)


def added(*parts):
    total = parts[0].astype(F32)
    for part in parts[1:]:
        total = total + part.astype(F32)
    return total


def scatter_dp_start(parts):
    one, two = lax.axis_index("dp") % 2, lax.axis_index("dp") // 2
    half = parts.shape[1] // 2
    grid = parts.reshape((2, 2) + parts.shape[1:])
    first, second = grid[:, :, :half], grid[:, :, half:]
    first_got = across(lax.dynamic_index_in_dim(first, 1 - one, 1, False), 1)
    second_got = across(lax.dynamic_index_in_dim(second, 1 - two, 0, False), 2)
    return grid, first_got, second_got


def scatter_middle_kernel(place_at, first, second, first_got, second_got, *outs):
    sums = (
        first[0, 0].astype(F32) + first_got[0].astype(F32),
        second[0, 0].astype(F32) + second_got[0].astype(F32),
    )

    def put(number):
        for way in range(2):
            outs[2 * number + way][...] = sums[way].astype(BF16)

    pl.when(pl.program_id(0) == 0)(lambda: put(0))
    pl.when(pl.program_id(0) != 0)(lambda: put(1))


def scatter_dp_middle(state):
    one, two = lax.axis_index("dp") % 2, lax.axis_index("dp") // 2
    grid, first_got, second_got = state
    shape = grid.shape[3:]
    half = (grid.shape[2] // 2,) + shape
    zeros = (0,) * len(shape)
    outs = pl.pallas_call(
        scatter_middle_kernel,
        grid_spec=pltpu.PrefetchScalarGridSpec(
            num_scalar_prefetch=1,
            grid=(2,),
            in_specs=[
                pl.BlockSpec((1, 1) + half, lambda i, p: (p[1] ^ 1 ^ i, p[0], 0) + zeros),
                pl.BlockSpec((1, 1) + half, lambda i, p: (p[1], p[0] ^ 1 ^ i, 1) + zeros),
                pl.BlockSpec((1,) + half, lambda i, p: (p[1] ^ 1 ^ i, 0) + zeros),
                pl.BlockSpec((1,) + half, lambda i, p: (p[0] ^ 1 ^ i, 0) + zeros),
            ],
            out_specs=[pl.BlockSpec(half, lambda i, p: (0,) + zeros)] * 4,
        ),
        out_shape=[jax.ShapeDtypeStruct(half, BF16)] * 4,
        compiler_params=pltpu.CompilerParams(vmem_limit_bytes=VMEM_LIMIT),
        cost_estimate=cheap(
            flops=2 * first_got.size, bytes_accessed=6 * grid.size, transcendentals=0
        ),
        name="scatter_middle",
    )(jnp.stack([one, two]), grid, grid, first_got, second_got)
    return outs[2], outs[3], across(outs[0], 2), across(outs[1], 1)


def scatter_dp_end(state, then=None):
    first_sum, second_sum, first_got, second_got = state
    if then is not None:
        first_got, second_got = tie(first_got, then), tie(second_got, then)
    return jnp.concatenate([added(first_sum, first_got), added(second_sum, second_got)], axis=0)


def gather_expert(block, by_hops):
    count = lax.axis_size("expert")
    if not by_hops:
        return lax.all_gather(block, "expert", axis=0)
    chip, core = lax.axis_index("expert") // 2, lax.axis_index("expert") % 2
    given = pair(block)
    both = jnp.where(core == 0, jnp.stack([block, given]), jnp.stack([given, block]))
    blocks = [both] + [hop(both, 2 * step) for step in range(1, count // 2)]
    pieces = []
    for place in range(count // 2):
        piece = blocks[0]
        for step in range(1, count // 2):
            piece = jnp.where((place + step) % (count // 2) == chip, blocks[step], piece)
        pieces.append(piece)
    return jnp.concatenate(pieces, axis=0)


def sum_over_chips(parts):
    chips = parts.shape[0]
    chip = lax.axis_index("expert") // 2
    got = [
        hop(lax.dynamic_index_in_dim(parts, (chip + step) % chips, 0, False), 2 * step)
        for step in range(1, chips)
    ]
    return added(lax.dynamic_index_in_dim(parts, chip, 0, False), *got).astype(BF16)


def spread_over_dp(owned):
    replicas, me = lax.axis_size("dp"), lax.axis_index("dp")
    blocks = [owned] + [across(owned, bits) for bits in range(1, replicas)]
    pieces = []
    for place_at in range(replicas):
        piece = blocks[0]
        for bits in range(1, replicas):
            piece = jnp.where(place_at ^ bits == me, blocks[bits], piece)
        pieces.append(piece.astype(F32))
    return jnp.concatenate(pieces, axis=0)


def standardised(values):
    center = values - jnp.mean(values, axis=-1, keepdims=True)
    spread = jnp.mean(center * center, axis=-1, keepdims=True)
    inverse = lax.rsqrt(spread + NORM_EPS)
    return center * inverse, inverse


def norm_pull(grad, unit, inverse, gain):
    scaled = grad * gain
    mean = jnp.mean(scaled, axis=-1, keepdims=True)
    along = jnp.mean(scaled * unit, axis=-1, keepdims=True)
    return inverse * (scaled - mean - unit * along)


def exact_gelu(values):
    return jax.nn.gelu(values, approximate=False)


def adam_step(weight, first, second, grad, rate, decay):
    new_first = BETA_ONE * first + (1.0 - BETA_ONE) * grad
    new_second = BETA_TWO * second + (1.0 - BETA_TWO) * grad * grad
    mean_hat = new_first / (1.0 - BETA_ONE**STEP)
    square_hat = new_second / (1.0 - BETA_TWO**STEP)
    updated = weight - rate * (mean_hat / (jnp.sqrt(square_hat) + ADAM_EPS) + decay * weight)
    return (new_first, new_second, updated)


def dot_nt(left, right):
    return lax.dot_general(left, right, (((1,), (1,)), ((), ())), preferred_element_type=F32)


def dot_tn(left, right):
    return lax.dot_general(left, right, (((0,), (0,)), ((), ())), preferred_element_type=F32)


def dot_nn(left, right):
    return jnp.dot(left, right, preferred_element_type=F32)


def by_head(block):
    first = lax.broadcasted_iota(jnp.int32, (1, LANES), 1) < HEAD_DIM
    return jnp.concatenate(
        [jnp.where(first, block, 0).astype(BF16), jnp.where(first, 0, block).astype(BF16)], axis=0
    )


def from_heads(turned):
    rows = turned.shape[1] // 2
    return jnp.concatenate([turned[:HEAD_DIM, :rows], turned[HEAD_DIM:, rows:]], axis=0).T


def window_of(starts, tile):
    return pl.ds(pl.multiple_of(starts[tile], 16), KEY_WINDOW)


def attend_tile(tile, window, query_image, key_image, q_ref, keys):
    low = tile * QUERY_TILE
    queries = by_head(q_ref[HALO + low : HALO + low + QUERY_TILE, :] * SCORE_SCALE)
    allowed = key_image[window, :] == query_image[:, low : low + QUERY_TILE]
    allowed = jnp.concatenate([allowed, allowed], axis=1)
    scores = jnp.where(allowed, dot_nt(keys, queries), MASKED)
    raised = jnp.exp(scores - jnp.max(scores, axis=0, keepdims=True))
    return queries, raised * (1.0 / jnp.sum(raised, axis=0, keepdims=True))


def attend_kernel(starts, query_image, key_image, q_ref, k_ref, v_ref, out_ref):
    for tile in range(out_ref.shape[0] // QUERY_TILE):
        window = window_of(starts, tile)
        _, attend = attend_tile(tile, window, query_image, key_image, q_ref, k_ref[window, :])
        found = dot_tn(v_ref[window, :], attend.astype(BF16))
        out_ref[tile * QUERY_TILE : (tile + 1) * QUERY_TILE, :] = from_heads(found).astype(BF16)


def image_specs(span, rows, blocks):
    return [
        pl.BlockSpec((1, rows), lambda i, t: (0, 0)),
        pl.BlockSpec((span, 1), lambda i, t: (0, 0)),
        pl.BlockSpec((span, LANES), lambda i, t: (0, i)),
        pl.BlockSpec((span, LANES), lambda i, t: (0, blocks + i)),
        pl.BlockSpec((span, LANES), lambda i, t: (0, 2 * blocks + i)),
    ]


def attention(triple, starts, query_image, key_image):
    span = triple.shape[0]
    rows = span - 2 * HALO
    width = triple.shape[1] // 3
    blocks = width // LANES
    cost = HEADS * rows * KEY_WINDOW
    return pl.pallas_call(
        attend_kernel,
        grid_spec=pltpu.PrefetchScalarGridSpec(
            num_scalar_prefetch=1,
            grid=(blocks,),
            in_specs=image_specs(span, rows, blocks),
            out_specs=pl.BlockSpec((rows, LANES), lambda i, t: (0, i)),
        ),
        out_shape=jax.ShapeDtypeStruct((rows, width), BF16),
        compiler_params=pltpu.CompilerParams(vmem_limit_bytes=VMEM_LIMIT),
        cost_estimate=cheap(
            flops=cost * 512, bytes_accessed=span * width * 6, transcendentals=cost
        ),
        name="attention",
    )(starts, query_image[None, :], key_image[:, None], triple, triple, triple)


def attend_back_kernel(
    starts, query_image, key_image, q_ref, k_ref, v_ref, g_ref, out_ref, dk, dv
):
    rows = g_ref.shape[0]
    span = k_ref.shape[0]
    width = out_ref.shape[1] // 3
    column = pl.program_id(0) * LANES

    def columns(part):
        return pl.ds(pl.multiple_of(part * width + column, LANES), LANES)

    dk[...] = jnp.zeros_like(dk)
    dv[...] = jnp.zeros_like(dv)
    out_ref[:HALO, columns(0)] = jnp.zeros((HALO, LANES), BF16)
    out_ref[span - HALO :, columns(0)] = jnp.zeros((HALO, LANES), BF16)
    for tile in range(rows // QUERY_TILE):
        low = tile * QUERY_TILE
        window = window_of(starts, tile)
        keys = k_ref[window, :]
        queries, attend = attend_tile(tile, window, query_image, key_image, q_ref, keys)
        grads = by_head(g_ref[low : low + QUERY_TILE, :])
        pulled = dot_nt(v_ref[window, :], grads)
        inner = jnp.sum(attend * pulled, axis=0, keepdims=True)
        score_grad = (attend * (pulled - inner)).astype(BF16)
        dv[window, :] += dot_nn(attend.astype(BF16), grads)
        dk[window, :] += dot_nn(score_grad, queries)
        query_grad = from_heads(dot_tn(keys, score_grad)) * SCORE_SCALE
        out_ref[HALO + low : HALO + low + QUERY_TILE, columns(0)] = query_grad.astype(BF16)
    out_ref[:, columns(1)] = dk[...].astype(BF16)
    out_ref[:, columns(2)] = dv[...].astype(BF16)


def attention_back(triple, grads, starts, query_image, key_image):
    span = triple.shape[0]
    rows = span - 2 * HALO
    width = triple.shape[1] // 3
    blocks = width // LANES
    cost = HEADS * rows * KEY_WINDOW
    return pl.pallas_call(
        attend_back_kernel,
        grid_spec=pltpu.PrefetchScalarGridSpec(
            num_scalar_prefetch=1,
            grid=(blocks,),
            in_specs=image_specs(span, rows, blocks)
            + [pl.BlockSpec((rows, LANES), lambda i, t: (0, i))],
            out_specs=pl.BlockSpec((span, 3 * width), lambda i, t: (0, 0)),
            scratch_shapes=[pltpu.VMEM((span, LANES), F32), pltpu.VMEM((span, LANES), F32)],
        ),
        out_shape=jax.ShapeDtypeStruct((span, 3 * width), BF16),
        compiler_params=pltpu.CompilerParams(vmem_limit_bytes=VMEM_LIMIT),
        cost_estimate=cheap(
            flops=cost * 1280, bytes_accessed=span * width * 14, transcendentals=cost
        ),
        name="attention_back",
    )(starts, query_image[None, :], key_image[:, None], triple, triple, triple, grads)


def first_norm_kernel(below, tokens, above, vectors, out):
    low = 0
    for block in (below, tokens, above):
        unit, _ = standardised(block[...].astype(F32))
        out[low : low + block.shape[0], :] = (unit * vectors[0:1] + vectors[1:2]).astype(BF16)
        low += block.shape[0]


def first_norm(below, tokens, above, vectors):
    span, width = tokens.shape[0] + 2 * HALO, tokens.shape[1]
    return pl.pallas_call(
        first_norm_kernel,
        out_shape=jax.ShapeDtypeStruct((span, width), BF16),
        compiler_params=pltpu.CompilerParams(vmem_limit_bytes=VMEM_LIMIT),
        cost_estimate=cheap(
            flops=span * width * 10, bytes_accessed=span * width * 4, transcendentals=0
        ),
        name="first_norm",
    )(below, tokens, above, vectors)


def second_norm_kernel(
    heads, weight, tokens, vectors, router, routes, resid_out, payload_out, gates_out
):
    rows, width = tokens.shape
    resid = tokens[...].astype(F32) + dot_nn(heads[...], weight[...])
    resid_out[...] = resid
    unit, _ = standardised(resid)
    hidden = (unit * vectors[0:1] + vectors[1:2]).astype(BF16)
    payload_out[:rows, :] = hidden
    logits = dot_nt(router[...], hidden)
    expert = lax.broadcasted_iota(jnp.int32, logits.shape, 0)
    named = (expert == routes[0:1]) | (expert == routes[1:2])
    peak = jnp.max(jnp.where(named, logits, -jnp.inf), axis=0, keepdims=True)
    raised = jnp.where(named, jnp.exp(jnp.where(named, logits - peak, 0.0)), 0.0)
    gates = raised / jnp.sum(raised, axis=0, keepdims=True)
    gates_out[...] = gates
    high = gates.astype(BF16).astype(F32)
    payload_out[rows:, :rows] = jnp.concatenate([high, gates - high], axis=0).astype(BF16)
    payload_out[rows:, rows:] = jnp.zeros((EXTRA, width - rows), BF16)


def second_norm(heads, weight, tokens, vectors, router, routes):
    rows, width = tokens.shape
    return pl.pallas_call(
        second_norm_kernel,
        out_shape=[
            jax.ShapeDtypeStruct((rows, width), F32),
            jax.ShapeDtypeStruct((rows + EXTRA, width), BF16),
            jax.ShapeDtypeStruct((8, rows), F32),
        ],
        compiler_params=pltpu.CompilerParams(vmem_limit_bytes=VMEM_LIMIT),
        cost_estimate=cheap(
            flops=2 * rows * width * width,
            bytes_accessed=rows * width * 10 + width * width * 2,
            transcendentals=0,
        ),
        name="second_norm",
    )(heads, weight, tokens, vectors, router, routes)


def dense_back_kernel(
    layout,
    me,
    hidden,
    below,
    tokens,
    above,
    grads,
    weight,
    heads,
    branch,
    small,
    give_out,
    keep_out,
    back_out,
):
    cores, replicas, chips, rows = layout
    width = hidden.shape[1]
    gain = jnp.zeros((1, width), F32)
    shift = jnp.zeros((1, width), F32)
    low = 0
    for block in (below, tokens, above):
        here = slice(low, low + block.shape[0])
        back = dot_nt(grads[here, :], weight[...])
        back_out[here, :] = back.astype(BF16)
        unit, _ = standardised(block[...].astype(F32))
        gain += jnp.sum(back * unit, axis=0, keepdims=True)
        shift += jnp.sum(back, axis=0, keepdims=True)
        low += block.shape[0]
    sums = jnp.concatenate(
        [
            gain,
            shift,
            jnp.zeros((6, width), F32),
        ],
        axis=0,
    )
    lane = lax.broadcasted_iota(jnp.int32, (8, LANES), 1)
    row = lax.broadcasted_iota(jnp.int32, (8, LANES), 0)
    spread = (lane == row).astype(F32)

    def store(low, block):
        for core in range(cores):

            def put(out, core=core):
                for chip in range(chips):
                    for replica in range(replicas):
                        start = ((chip * cores + core) * replicas + replica) * rows
                        piece = block[start : start + rows].astype(BF16)
                        out[replica, chip, :, low : low + block.shape[1]] = piece

            pl.when(me[0] == core)(lambda: put(keep_out))
            pl.when(me[0] != core)(lambda: put(give_out))

    for low in range(0, 3 * width, width):
        store(low, dot_tn(hidden[...], grads[:, low : low + width]))
    store(3 * width, dot_tn(heads[...], branch[...]))
    store(
        4 * width,
        lax.dot_general(
            small[...] + sums,
            spread,
            (((0,), (0,)), ((), ())),
            precision=HIGHEST,
            preferred_element_type=F32,
        ),
    )


def dense_back(hidden, below, tokens, above, grads, weight, heads, branch, small, layout):
    span, width = hidden.shape
    columns = 4 * width + LANES
    core = lax.axis_index("expert") % 2
    return pl.pallas_call(
        functools.partial(dense_back_kernel, layout),
        out_shape=[
            jax.ShapeDtypeStruct(layout[1:] + (columns,), BF16),
            jax.ShapeDtypeStruct(layout[1:] + (columns,), BF16),
            jax.ShapeDtypeStruct((span, width), BF16),
        ],
        in_specs=[pl.BlockSpec(memory_space=pltpu.SMEM)]
        + [pl.BlockSpec(memory_space=pltpu.VMEM)] * 9,
        compiler_params=pltpu.CompilerParams(vmem_limit_bytes=VMEM_LIMIT),
        cost_estimate=cheap(
            flops=span * width * width * 12,
            bytes_accessed=span * width * 16 + width * width * 12,
            transcendentals=0,
        ),
        name="dense_back",
    )(core.reshape(1), hidden, below, tokens, above, grads, weight, heads, branch, small)


def small_adam_kernel(sums, *refs):
    values = [ref[...] for ref in refs[:6]]
    vectors, matrix = refs[0].shape[0], refs[3].shape[0]
    rows = sums.shape[0]
    lane = lax.broadcasted_iota(jnp.int32, (rows, rows), 1)
    row = lax.broadcasted_iota(jnp.int32, (rows, rows), 0)
    turned = lax.dot_general(
        sums[...],
        (lane == row).astype(F32),
        (((0,), (0,)), ((), ())),
        precision=HIGHEST,
        preferred_element_type=F32,
    )
    found = adam_step(*values[:3], turned[:vectors], VECTOR_RATE, 0.0)
    found += adam_step(*values[3:], turned[vectors : vectors + matrix], MATRIX_RATE, DECAY)
    for ref, value in zip(refs[6:], found):
        ref[...] = value


def small_adam(sums, *arrays):
    return pl.pallas_call(
        small_adam_kernel,
        out_shape=[jax.ShapeDtypeStruct(array.shape, F32) for array in arrays],
        name="small_adam",
    )(sums, *arrays)


def gelu_and_slope(values):
    inverse = 1.0 / (1.0 + (0.3275911 * 0.7071067811865476) * jnp.abs(values))
    fit = 1.061405429 * inverse - 1.453152027
    fit = fit * inverse + 1.421413741
    fit = fit * inverse - 0.284496736
    fit = fit * inverse + 0.254829592
    bell = jnp.exp(-0.5 * values * values)
    tail = (0.5 * fit) * (inverse * bell)
    share = jnp.where(values >= 0.0, 1.0 - tail, tail)
    return values * share, share + values * (bell * 0.3989422804014327)


def expert_kernel(first, target, rows_ref, grads_ref, gates, mark, place, weights, *refs):
    outs = refs if first else refs[5:]
    act_out, pre_out, part_out, rows_out, mixed_out, back_out = outs
    tile = pl.program_id(0)
    rows = rows_ref[...]
    gate = dot_tn(gates[...], mark[...])
    width = rows.shape[1]
    gate = jnp.concatenate([gate] * (width // LANES), axis=1)
    grads_float = grads_ref[...].astype(F32)
    grad_part = (gate * grads_float).astype(BF16)
    rows_out[...] = rows
    part_out[...] = grad_part
    part = None
    back = None
    replicas, parts, size = weights.shape
    quarter = parts // 4
    narrow_all = weights[:, 2 * quarter :, :].reshape(2 * size, width)
    for turn in range(2):
        here = slice(turn * size, (turn + 1) * size)
        widen = weights[:, turn * quarter : (turn + 1) * quarter, :].reshape(width, size)
        narrow = narrow_all[here, :]
        before = dot_nn(rows, widen)
        pulled = dot_nt(grad_part, narrow)
        act, slope = gelu_and_slope(before)
        act = act.astype(BF16)
        grad_pre = (pulled * slope).astype(BF16)
        act_out[:, here] = act
        pre_out[:, here] = grad_pre
        part_here = dot_nn(act, narrow)
        back_here = dot_nt(grad_pre, widen)
        part = part_here if part is None else part + part_here
        back = back_here if back is None else back + back_here
    part = part.astype(BF16).astype(F32)
    product = part * grads_float
    folded = product[:, :LANES]
    for low in range(LANES, width, LANES):
        folded = folded + product[:, low : low + LANES]
    dots = lax.dot_general(
        jnp.ones((EXTRA, LANES), F32),
        folded,
        (((1,), (1,)), ((), ())),
        precision=HIGHEST,
        preferred_element_type=F32,
    )
    high = dots.astype(BF16).astype(F32)
    dots = high * place[0] + (dots - high) * place[1]
    mixed_out[...] = (gate * part).astype(BF16)
    count = rows.shape[0]
    back_out[pl.ds(pl.multiple_of(tile * count, count), count), :] = back.astype(BF16)
    extra = slice(back_out.shape[0] - EXTRA, back_out.shape[0])
    back_out[extra, pl.ds(pl.multiple_of(tile * count, count), count)] = dots.astype(BF16)


def expert_block(place, places, target, payload, grads_block, marks, weights, kept):
    rows, width = grads_block.shape
    replicas, parts, _ = weights.shape
    hidden = parts * replicas // 2
    tiles = rows // ROW_TILE
    every = places * rows
    by_tile = pl.BlockSpec((ROW_TILE, width), lambda i, t: (i, 0))
    at = lambda i, t: (place * tiles + i, 0)
    whole = lambda i, t: (0, 0)
    first = kept is None
    kept = () if first else kept
    gate_mark, dot_mark = marks
    return pl.pallas_call(
        functools.partial(expert_kernel, first),
        grid_spec=pltpu.PrefetchScalarGridSpec(
            num_scalar_prefetch=1,
            grid=(tiles,),
            in_specs=[
                by_tile,
                by_tile,
                pl.BlockSpec((EXTRA, ROW_TILE), lambda i, t: (rows // EXTRA, i)),
                pl.BlockSpec((EXTRA, LANES), whole),
                pl.BlockSpec((2, EXTRA, 1), lambda i, t: (0, 0, 0)),
                pl.BlockSpec(
                    (replicas, parts, width), lambda i, t: (0, 0, 0), pipeline_mode=pl.Buffered(1)
                ),
            ]
            + [pl.BlockSpec(memory_space=pl.ANY)] * len(kept),
            out_specs=[
                pl.BlockSpec((ROW_TILE, hidden), at),
                pl.BlockSpec((ROW_TILE, hidden), at),
                pl.BlockSpec((ROW_TILE, width), at),
                pl.BlockSpec((ROW_TILE, width), at),
                pl.BlockSpec((ROW_TILE, width), lambda i, t: (t[0] * tiles + i, 0)),
                pl.BlockSpec((rows + EXTRA, width), whole),
            ],
        ),
        out_shape=[
            pltpu.HBM((every, hidden), BF16),
            pltpu.HBM((every, hidden), BF16),
            pltpu.HBM((every, width), BF16),
            pltpu.HBM((every, width), BF16),
            pltpu.HBM((every, width), BF16),
            jax.ShapeDtypeStruct((rows + EXTRA, width), BF16),
        ],
        input_output_aliases={7 + i: i for i in range(len(kept))},
        compiler_params=pltpu.CompilerParams(vmem_limit_bytes=EXPERT_VMEM),
        cost_estimate=cheap(
            flops=rows * width * hidden * 8,
            bytes_accessed=rows * (2 * hidden + 6 * width) * 2 + 4 * width * hidden,
            transcendentals=rows * hidden,
        ),
        name="expert_block",
    )(
        target.reshape(1),
        payload,
        grads_block,
        payload,
        gate_mark,
        dot_mark,
        weights,
        *kept,
    )


def experts_by_ring(payload, expert_count, weights, next_grads, grads_mine):
    chips = lax.axis_size("expert") // 2
    rows = payload.shape[0] - EXTRA
    chip, core = lax.axis_index("expert") // 2, lax.axis_index("expert") % 2
    number = jnp.arange(EXTRA, dtype=jnp.int32)[:, None]
    gate_mark = jnp.broadcast_to(number % 8 == chip, (EXTRA, LANES)).astype(BF16)
    slot = 2 * (core * expert_count + chip)
    dot_mark = jnp.stack([number == slot, number == slot + 1]).astype(F32)
    marks = (gate_mark, dot_mark)
    kept = None
    carry = None
    backs = []
    mine = payload
    for step in range(chips):
        other = pair(mine)
        if step + 1 < chips:
            following = ring(mine)
        source = (chip - step) % chips
        found_mine = expert_block(
            2 * step,
            2 * chips,
            2 * source + core,
            mine,
            grads_mine[step],
            marks,
            weights,
            kept,
        )
        found_other = expert_block(
            2 * step + 1,
            2 * chips,
            2 * source + 1 - core,
            other,
            pair(grads_mine[step]),
            marks,
            weights,
            found_mine[:5],
        )
        kept = found_other[:5]
        next_grads(found_other[5])
        backs.append((found_mine[5], found_other[5]))
        if step:
            terms = [backs[step][0], pair(backs[step][1])] + ([] if step == 1 else [carry])
            total = added(*terms).astype(BF16)
            carry = ring(total)
        if step + 1 < chips:
            mine = tie(following, found_other[5], *grads_mine[step + 1 :])
    act_all, pre_all, part_all, rows_all, outs = kept
    rows_all, act_all = tie(rows_all, total), tie(act_all, total)
    grad_widen = dot_tn(rows_all, pre_all).astype(BF16)
    grad_narrow = dot_tn(act_all, part_all).astype(BF16)
    grad_all = added(backs[0][0], pair(backs[0][1]), tie(carry, grad_widen, grad_narrow))
    outs = tie(outs, total)
    grad_hidden = grad_all[:rows]
    table = grad_all[rows : rows + 4 * expert_count, :rows]
    table = jnp.sum(table.reshape(2, expert_count, 2, rows), axis=(0, 2))
    return outs, table, grad_hidden, grad_widen, grad_narrow


def slot_layout(routes, expert_count):
    flat = routes.reshape(-1)
    table = (flat[:, None] == jnp.arange(expert_count, dtype=jnp.int32)[None, :]).astype(jnp.int32)
    before = jnp.cumsum(table, axis=0) - table
    return (flat, jnp.sum(before * table, axis=1))


def to_experts(buffer):
    doubled = jnp.repeat(buffer, 2, axis=0)
    return lax.all_to_all(doubled, "expert", split_axis=0, concat_axis=0, tiled=True)


def both_halves(received, expert_ids, slot_ids):
    slices, capacity, width = received.shape
    summed = jnp.sum(received.astype(F32).reshape(slices // 2, 2, capacity, width), axis=1)
    return summed[expert_ids, slot_ids]


def experts_by_slots(hidden_two, cotangent, routes, gates_table, widen_low, narrow_low, capacity):
    expert_count = gates_table.shape[0]
    device_count = lax.axis_size("expert")
    rows_dev, width = hidden_two.shape
    chooser = (
        routes[:, :, None] == jnp.arange(expert_count, dtype=jnp.int32)[None, None, :]
    ).astype(F32)
    gates = jnp.sum(chooser * gates_table.T[:, None, :], axis=-1)
    expert_ids, slot_ids = slot_layout(routes, expert_count)
    dispatch = (
        jnp.zeros((expert_count, capacity, width), BF16)
        .at[expert_ids, slot_ids]
        .set(jnp.repeat(hidden_two, 2, axis=0))
    )
    expert_rows = to_experts(dispatch).reshape(device_count * capacity, width)
    before_act = dot_nn(expert_rows, widen_low)
    act_low = exact_gelu(before_act).astype(BF16)
    parts_low = dot_nn(act_low, narrow_low).astype(BF16).reshape(device_count, capacity, width)
    returned = lax.all_to_all(parts_low, "expert", split_axis=0, concat_axis=0, tiled=True)
    combined = both_halves(returned, expert_ids, slot_ids).reshape(rows_dev, 2, width)
    out = jnp.sum(gates[:, :, None] * combined, axis=1)
    grad_output = cotangent.astype(F32)
    grad_parts = (
        (gates[:, :, None] * grad_output[:, None, :]).astype(BF16).reshape(2 * rows_dev, width)
    )
    grad_dispatch = (
        jnp.zeros((expert_count, capacity, width), BF16).at[expert_ids, slot_ids].set(grad_parts)
    )
    grad_rows = to_experts(grad_dispatch).reshape(device_count * capacity, width)
    grad_act = dot_nt(grad_rows, narrow_low)
    grad_before = jax.vjp(exact_gelu, before_act)[1](grad_act)[0].astype(BF16)
    grad_narrow = dot_tn(act_low, grad_rows).astype(BF16)
    grad_widen = dot_tn(expert_rows, grad_before).astype(BF16)
    grad_back = dot_nt(grad_before, widen_low).reshape(device_count, capacity, width)
    grad_returned = lax.all_to_all(
        grad_back.astype(BF16), "expert", split_axis=0, concat_axis=0, tiled=True
    )
    grad_hidden = jnp.sum(
        both_halves(grad_returned, expert_ids, slot_ids).reshape(rows_dev, 2, width), axis=1
    )
    grad_gates = jnp.sum(grad_output[:, None, :] * combined, axis=-1)
    table = jnp.sum(grad_gates[:, :, None] * chooser, axis=1).T
    return out, table, grad_hidden, grad_widen, grad_narrow


def local(
    tokens,
    cotangent,
    routes,
    attention_weight,
    attention_first,
    attention_second,
    router_weight,
    router_first,
    router_second,
    norm_vectors,
    norm_first,
    norm_second,
    widen_weight,
    widen_first,
    widen_second,
    narrow_weight,
    narrow_first,
    narrow_second,
):
    device_count = lax.axis_size("expert")
    replicas = lax.axis_size("dp")
    expert_count = device_count // 2
    rows_dev, width = tokens.shape
    capacity = min(rows_dev, 4 * rows_dev // expert_count)
    by_ring = capacity == rows_dev and replicas == 4
    device = lax.axis_index("expert")

    attention_cast = attention_weight.astype(BF16)
    small_own = jnp.concatenate(
        [router_weight.astype(BF16).T, norm_vectors.astype(BF16)], axis=0
    )
    triple_weight = lax.all_gather(attention_cast[:, : 3 * width], "expert", axis=0, tiled=True)
    small_low = gather_expert(small_own, by_ring).transpose(1, 0, 2).reshape(-1, width)
    proj_weight = lax.all_gather(attention_cast[:, 3 * width :], "expert", axis=0, tiled=True)
    router_low = small_low[:expert_count]
    norm_float = small_low[expert_count:].astype(F32)

    widen_cast, narrow_cast = widen_weight[0].astype(BF16), narrow_weight[0].astype(BF16)
    if by_ring:
        half = widen_cast.shape[1] // 2
        halves = jnp.concatenate(
            [widen_cast[:, :half], widen_cast[:, half:], narrow_cast], axis=0
        )
        experts_near, experts_far = gather_dp_near(halves)
    else:
        widen_low = lax.all_gather(widen_cast, "dp", axis=0, tiled=True)
        narrow_low = lax.all_gather(narrow_cast, "dp", axis=0, tiled=True)

    grads_mine = [cotangent]

    def next_grads(*dependencies):
        if by_ring and len(grads_mine) < expert_count:
            grads_mine[-1] = tie(grads_mine[-1], *dependencies)
            grads_mine.append(ring(grads_mine[-1]))

    next_grads(small_low)

    below = lax.ppermute(
        tokens[rows_dev - HALO :], "expert", [(i, i + 1) for i in range(device_count - 1)]
    )
    above = lax.ppermute(
        tokens[:HALO], "expert", [(i + 1, i) for i in range(device_count - 1)]
    )
    if by_ring:
        below = tie(below, experts_near)
    hidden_one = first_norm(below, tokens, above, norm_float[:2])
    next_grads(hidden_one, triple_weight)
    triple = dot_nn(hidden_one, triple_weight).astype(BF16)
    first_row = device * rows_dev
    query_rows = first_row + jnp.arange(rows_dev, dtype=jnp.int32)
    key_rows = first_row - HALO + jnp.arange(rows_dev + 2 * HALO, dtype=jnp.int32)
    query_image = query_rows // SEQ
    inside = (key_rows >= 0) & (key_rows < rows_dev * device_count)
    key_image = jnp.where(inside, key_rows // SEQ, -1)
    tile_rows = first_row + QUERY_TILE * jnp.arange(rows_dev // QUERY_TILE, dtype=jnp.int32)
    starts = tile_rows // SEQ * SEQ - (first_row - HALO)
    starts = jnp.minimum(starts // 16 * 16, rows_dev + 2 * HALO - KEY_WINDOW)
    heads_low = attention(triple, starts, query_image, key_image)
    if by_ring:
        expert_weights = gather_dp_far(experts_near, tie(experts_far, heads_low))
    tokens_float = tokens.astype(F32)
    if by_ring:
        router_rows = jnp.pad(router_low, ((0, 8 - expert_count), (0, 0)))
        resid, payload, gates = second_norm(
            heads_low, proj_weight, tokens, tie(norm_float[2:], expert_weights), router_rows, routes.T
        )
        gates = gates[:expert_count]
        payload = tie(payload, grads_mine[-1])
        next_grads(payload)
        hidden_two = payload[:rows_dev]
        unit_two, inverse_two = standardised(resid)
    else:
        resid = tokens_float + dot_nn(heads_low, proj_weight)
        unit_two, inverse_two = standardised(resid)
        hidden_two = (unit_two * norm_float[2] + norm_float[3]).astype(BF16)
        logits = dot_nt(router_low, hidden_two)
        experts = jnp.arange(expert_count, dtype=jnp.int32)[:, None]
        named = (routes[:, 0][None, :] == experts) | (routes[:, 1][None, :] == experts)
        peak = jnp.max(jnp.where(named, logits, -jnp.inf), axis=0, keepdims=True)
        raised = jnp.where(named, jnp.exp(jnp.where(named, logits - peak, 0.0)), 0.0)
        gates = raised / jnp.sum(raised, axis=0, keepdims=True)

    if by_ring:
        out, grad_gates, grad_hidden, grad_widen, grad_narrow = experts_by_ring(
            payload, expert_count, expert_weights, next_grads, grads_mine
        )
    else:
        out, grad_gates, grad_hidden, grad_widen, grad_narrow = experts_by_slots(
            hidden_two, cotangent, routes, gates, widen_low, narrow_low, capacity
        )
    if by_ring:
        scattered = [
            scatter_dp_start(grad.reshape(replicas, grad.shape[0] // replicas, grad.shape[1]))
            for grad in (grad_widen, grad_narrow)
        ]

    grad_logits = gates * (grad_gates - jnp.sum(gates * grad_gates, axis=0, keepdims=True))
    grad_router = lax.dot_general(
        grad_logits,
        hidden_two.astype(F32),
        (((1,), (0,)), ((), ())),
        precision=HIGHEST,
        preferred_element_type=F32,
    )
    grad_hidden = grad_hidden + lax.dot_general(
        grad_logits,
        router_low.astype(F32),
        (((0,), (0,)), ((), ())),
        precision=HIGHEST,
        preferred_element_type=F32,
    )
    grad_gain_two = jnp.sum(grad_hidden * unit_two, axis=0)
    grad_shift_two = jnp.sum(grad_hidden, axis=0)
    grad_resid = cotangent.astype(F32) + norm_pull(
        grad_hidden, unit_two, inverse_two, norm_float[2]
    )
    grad_branch = grad_resid.astype(BF16)
    grad_heads = dot_nt(grad_branch, proj_weight).astype(BF16)

    grad_triple = attention_back(triple, grad_heads, starts, query_image, key_image)
    if by_ring:
        scattered = [
            scatter_dp_middle((grid, tie(first, grad_triple), tie(second, grad_triple)))
            for grid, first, second in scattered
        ]
        grad_triple = tie(grad_triple, *(part for state in scattered for part in state[:2]))
    by_owner = (2, replicas, expert_count, width // (device_count * replicas))
    small_rows = jnp.concatenate(
        [
            jnp.zeros((2, width), F32),
            jnp.stack([grad_gain_two, grad_shift_two]),
            grad_router,
        ],
        axis=0,
    )
    if by_ring:
        grad_give, grad_keep, grad_hidden_one = dense_back(
            hidden_one,
            below,
            tokens,
            above,
            grad_triple,
            triple_weight,
            heads_low,
            grad_branch,
            small_rows,
            by_owner,
        )
        out = lax.psum_scatter(out, "expert", scatter_dimension=0, tiled=True)
        over_pair = added(grad_keep, pair(tie(grad_give, out))).astype(BF16)
        halfway = scatter_dp_middle(scatter_dp_start(over_pair))
        over_dp = scatter_dp_end(halfway)
        over_dp = over_dp.astype(BF16)
        owned = sum_over_chips(over_dp)
        dense_sum = spread_over_dp(owned)
        widen_sum, narrow_sum = [scatter_dp_end(state, halfway[0]) for state in scattered]
        out = tie(out, owned)
        attention_sum = dense_sum[:, : 4 * width]
        small_sum = dense_sum[:, 4 * width :]
    else:
        grad_hidden_one = dot_nt(grad_triple, triple_weight)
        extended = jnp.concatenate([below, tokens, above], axis=0).astype(F32)
        unit_one, _ = standardised(extended)
        small_rows = small_rows.at[0].set(jnp.sum(grad_hidden_one * unit_one, axis=0))
        small_rows = small_rows.at[1].set(jnp.sum(grad_hidden_one, axis=0))
        grad_hidden_one = grad_hidden_one.astype(BF16)
        grad_dense = jnp.concatenate(
            [
                dot_tn(hidden_one, grad_triple).astype(BF16),
                dot_tn(heads_low, grad_branch).astype(BF16),
                small_rows.T.astype(BF16),
            ],
            axis=1,
        )
        widen_sum = lax.psum_scatter(
            grad_widen, "dp", scatter_dimension=0, tiled=True
        ).astype(F32)
        narrow_sum = lax.psum_scatter(
            grad_narrow, "dp", scatter_dimension=0, tiled=True
        ).astype(F32)
        dense_sum = lax.psum(
            lax.psum_scatter(grad_dense, "expert", scatter_dimension=0, tiled=True), "dp"
        ).astype(F32)
        attention_sum = dense_sum[:, : 4 * width]
        small_sum = dense_sum[:, 4 * width :]
    from_above = lax.ppermute(
        grad_hidden_one[:HALO], "expert", [(i + 1, i) for i in range(device_count - 1)]
    )
    from_below = lax.ppermute(
        grad_hidden_one[rows_dev + HALO :],
        "expert",
        [(i, i + 1) for i in range(device_count - 1)],
    )
    if by_ring:
        from_above = tie(from_above, over_dp)
    grad_own = added(
        grad_hidden_one[HALO : HALO + rows_dev],
        jnp.concatenate([from_below, from_above], axis=0),
    )
    unit_one, inverse_one = standardised(tokens_float)
    tokens_grad = grad_resid + norm_pull(grad_own, unit_one, inverse_one, norm_float[0])

    if by_ring:
        out = out.astype(F32)
    mixed = (resid + out).astype(BF16)
    attention_new = adam_step(
        attention_weight, attention_first, attention_second, attention_sum, MATRIX_RATE, DECAY
    )
    if by_ring:
        small_new = small_adam(
            small_sum,
            norm_vectors,
            norm_first,
            norm_second,
            router_weight.T,
            router_first.T,
            router_second.T,
        )
        norm_new = tuple(small_new[:3])
        router_new = tuple(array.T for array in small_new[3:])
    else:
        norm_new = adam_step(
            norm_vectors, norm_first, norm_second, small_sum[:, :4].T, VECTOR_RATE, 0.0
        )
        router_new = adam_step(
            router_weight, router_first, router_second, small_sum[:, 4:], MATRIX_RATE, DECAY
        )
    widen_new = adam_step(
        widen_weight, widen_first, widen_second, widen_sum[None], MATRIX_RATE, DECAY
    )
    narrow_new = adam_step(
        narrow_weight, narrow_first, narrow_second, narrow_sum[None], MATRIX_RATE, DECAY
    )
    return (mixed, tokens_grad) + attention_new + router_new + norm_new + widen_new + narrow_new


def solution(mesh):
    rows = P(("dp", "expert"), None)
    dense = P("expert", None)
    vectors = P(None, "expert")
    halves = P("expert", "dp", None)
    return jax.shard_map(
        local,
        mesh=mesh,
        in_specs=(rows,) * 3 + (dense,) * 6 + (vectors,) * 3 + (halves,) * 6,
        out_specs=(rows,) * 2 + (dense,) * 6 + (vectors,) * 3 + (halves,) * 6,
        check_vma=False,
    )
```
